32 devices in a mesh: row: 4 (over z), col: 8 (over y, x, core).
Axes of the slice: x: 2, y: 2, z: 4, core: 2. Of those that a mesh axis runs over, the one named last changes fastest.
Arguments:
- iterate: float32 [256, 16384], P('row', 'col'), may hold values from -6 to 6
- residual: float32 [256, 16384], P('row', 'col'), may hold values from -24 to 24
- direction: float32 [256, 16384], P('row', 'col'), may hold values from -24 to 24
- window_weight: float32 [16, 1024], P('row', 'col'), may hold values from 0.2 to 5
- freq_weight: float32 [32, 32], replicated, may hold values from 0.2 to 5
Outputs:
- new_iterate: float32 [256, 16384], P('row', 'col')
- new_residual: float32 [256, 16384], P('row', 'col')
- new_direction: float32 [256, 16384], P('row', 'col')
The draws below stay inside these ranges and needn't reach their ends.
All inputs are finite; a program needn't handle non-finite values.
Results may differ from the reference program's by a relative error of at most 0.0003.
Values sent between devices are 32-bit elements; how exact they have to be, the bound alone decides.
A program may use at most 64 MiB of HBM per device.

```python
import math
import jax
import jax.numpy as jnp
from jax import lax

CD = 2048
NR = 256
NC = 16384
N_COL = 8


def rising_field(key):
    column_pos = jnp.arange(NC, dtype=jnp.float32)
    column_ramp = 1.0 + 2.0 * column_pos / NC
    first_key = jax.random.fold_in(key, 0)
    entries = jnp.clip(jax.random.normal(first_key, (NR, NC), jnp.float32), -4.0, 4.0)
    return entries * column_ramp[None, :]


def draw_residual(key, part):
    return rising_field(jax.random.fold_in(key, 11))


def draw_direction(key, part):
    return rising_field(jax.random.fold_in(key, 23))


def level_of(key, dims, shards, smallest, largest):
    gain = 1.0
    for position, blocks in shards:
        steps = jax.random.uniform(jax.random.fold_in(jax.random.fold_in(key, 6), position), (blocks,), jnp.float32, smallest / len(shards), largest / len(shards))
        gain = gain * jnp.repeat(jnp.exp(steps), dims[position] // blocks).reshape((-1,) + (1,) * (len(dims) - 1 - position))
    return gain


def noise(stream_key, dims, scale, reach, shards=(), kind=jnp.bfloat16):
    drawn = jax.random.normal(stream_key, dims, jnp.float32) * scale
    if len(shards) > 0:
        drawn = level_of(stream_key, dims, shards, -0.22, 0.18) * drawn
    return jnp.clip(drawn, min=-reach, max=reach).astype(kind)


def setup_inputs(seed: int = 0) -> dict:
    keys = jax.random.split(jax.random.key(seed), 6)
    iterate = noise(keys[0], (NR, NC), 1.0, 6.0, ((0, 4), (1, 8)), jnp.float32)
    residual = draw_residual(jax.random.fold_in(keys[5], 71), 0)
    direction = draw_direction(jax.random.fold_in(keys[5], 71), 0)
    window_weight = jnp.clip(jnp.exp(math.log(5.0) - 3.218876 * jax.random.uniform(keys[3], (NR // 16, NC // 16), jnp.float32) ** level_of(keys[3], (NR // 16, NC // 16), ((0, 4), (1, 8)), -0.2, 0.2)), 0.2, 5.0)
    freq_weight = jnp.clip(jnp.exp(jax.random.uniform(keys[4], (32, 32), jnp.float32, math.log(0.2), math.log(5.0))), 0.2, 5.0)
    return {"iterate": iterate, "residual": residual, "direction": direction, "window_weight": window_weight, "freq_weight": freq_weight}


precise = lax.Precision.HIGHEST
damping = 0.5

def tables():
    positions = jnp.arange(32, dtype=jnp.float32)
    window = jnp.exp(-0.5 * ((positions - 15.5) / 8.0) ** 2)
    phases = 2.0 * jnp.pi * jnp.outer(positions, positions) / 32.0
    cos_part = jnp.cos(phases) * window[None, :] / jnp.sqrt(32.0)
    sin_part = -jnp.sin(phases) * window[None, :] / jnp.sqrt(32.0)
    column_table = jnp.concatenate([cos_part.T, sin_part.T], axis=1)
    cos_split = cos_part.reshape(32, 2, 16)
    sin_split = sin_part.reshape(32, 2, 16)
    upper = jnp.stack([cos_split, -sin_split], axis=-1)
    lower = jnp.stack([sin_split, cos_split], axis=-1)
    row_table = jnp.concatenate([upper, lower], axis=0).reshape(64, 64)
    return (column_table, row_table)

def analyze(region, column_table, row_table):
    win_rows = region.shape[0] // 16 - 1
    win_cols = region.shape[1] // 16 - 1
    blocks = region.reshape(win_rows + 1, 16, win_cols + 1, 16)
    section_one = jnp.einsum('akbl,lp->akpb', blocks[:, :, :win_cols], column_table[:16], precision=precise)
    section_one = section_one + jnp.einsum('akbl,lp->akpb', blocks[:, :, 1:], column_table[16:], precision=precise)
    section_one = section_one.reshape(win_rows + 1, 16, 2, 32, win_cols)
    paired = jnp.stack([section_one[:-1], section_one[1:]], axis=1).reshape(win_rows, 64, 32, win_cols)
    return jnp.einsum('tm,amvb->atvb', row_table, paired, precision=precise)

def weigh(coefficients, window_weight, freq_weight):
    doubled = jnp.concatenate([freq_weight, freq_weight], axis=0)
    return coefficients * doubled[None, :, :, None] * window_weight[:, None, None, :]

def synthesize(coefficients, column_table, row_table):
    win_rows = coefficients.shape[0]
    win_cols = coefficients.shape[3]
    spread = jnp.einsum('tm,atvb->amvb', row_table, coefficients, precision=precise)
    spread = spread.reshape(win_rows, 2, 16, 64, win_cols)
    stacked = jnp.pad(spread[:, 0], ((0, 1), (0, 0), (0, 0), (0, 0))) + jnp.pad(spread[:, 1], ((1, 0), (0, 0), (0, 0), (0, 0)))
    lower_piece = jnp.einsum('akpb,lp->akbl', stacked, column_table[:16], precision=precise)
    upper_piece = jnp.einsum('akpb,lp->akbl', stacked, column_table[16:], precision=precise)
    blocks = jnp.pad(lower_piece, ((0, 0), (0, 0), (0, 1), (0, 0))) + jnp.pad(upper_piece, ((0, 0), (0, 0), (1, 0), (0, 0)))
    return blocks.reshape(16 * (win_rows + 1), 16 * (win_cols + 1))

def apply_normal(vector, window_weight, freq_weight):
    column_table, row_table = tables()
    padded = jnp.pad(vector, ((0, 16), (0, 16)))

    def one_block(block_index):
        start = (block_index * CD).astype(jnp.int32)
        region = lax.dynamic_slice(padded, (jnp.int32(0), start), (NR + 16, CD + 16))
        weight_start = (block_index * (CD // 16)).astype(jnp.int32)
        weights_here = lax.dynamic_slice(window_weight, (jnp.int32(0), weight_start), (NR // 16, CD // 16))
        coefficients = weigh(analyze(region, column_table, row_table), weights_here, freq_weight)
        return synthesize(coefficients, column_table, row_table)
    pieces = lax.map(one_block, jnp.arange(N_COL, dtype=jnp.int32))
    main_part = pieces[:, :, :CD].transpose(1, 0, 2).reshape(NR + 16, NC)
    tail_rows = jnp.pad(pieces[:-1, :, CD:].transpose(1, 0, 2), ((0, 0), (1, 0), (0, CD - 16))).reshape(NR + 16, NC)
    return (main_part + tail_rows)[:NR] + damping * vector

def reference(iterate, residual, direction, window_weight, freq_weight):
    norm_now = jnp.sum(residual * residual)
    applied = apply_normal(direction, window_weight, freq_weight)
    curvature = jnp.sum(direction * applied)
    step_length = norm_now / curvature
    new_iterate = iterate + step_length * direction
    new_residual = residual - step_length * applied
    norm_next = jnp.sum(new_residual * new_residual)
    new_direction = new_residual + norm_next / norm_now * direction
    return (new_iterate, new_residual, new_direction)
```

```python
import functools

import jax
import jax.numpy as jnp
import ml_dtypes
import numpy as np
from jax import lax
from jax.experimental import pallas as pl
from jax.experimental.pallas import tpu as pltpu
from jax.sharding import PartitionSpec as P

MESH = pl.DeviceIdType.MESH
damping = 0.5


def split_host(table):
    table = np.asarray(table, np.float32)
    high = table.astype(ml_dtypes.bfloat16)
    low = (table - high.astype(np.float32)).astype(ml_dtypes.bfloat16)
    return jnp.asarray(high), jnp.asarray(low)


def host_tables(win_rows):
    j = np.arange(32)
    window = np.exp(-0.5 * ((j - 15.5) / 8.0) ** 2)
    basis = np.zeros((2, 16, 32))
    for w in range(16):
        phase = 2.0 * np.pi * w * j / 32.0
        basis[0, w] = np.sqrt(2.0) * np.cos(phase) if w else 1.0
        basis[1, w] = np.sqrt(2.0) * np.sin(phase) if w else (-1.0) ** j
    basis = basis * window / np.sqrt(32.0)
    col = np.zeros((256, 2, 16, 8))
    for b in range(8):
        col[112 + 16 * b : 144 + 16 * b, :, :, b] = basis.transpose(2, 0, 1)
    col = col.reshape(256, 256)
    height = 16 * win_rows
    row = np.zeros((32 * (win_rows + 1), height + 32))
    for a in range(win_rows + 1):
        row[32 * a : 32 * a + 32, 16 * a : 16 * a + 32] = basis.reshape(32, 32)
    row_back = row.T[16 : 16 + height]
    even = np.zeros((2, 16, 32))
    odd = np.zeros((2, 16, 32))
    for h in range(2):
        for w in range(16):
            f = 16 if (h == 1 and w == 0) else w
            even[h, w, f] += 0.5
            even[h, w, -f % 32] += 0.5
            sign = 1.0 - 2.0 * h
            odd[h, w, f] += 0.5 * sign
            odd[h, w, -f % 32] -= 0.5 * sign
    even, odd = even.reshape(32, 32), odd.reshape(32, 32)
    left = np.stack([even, -odd]).astype(np.float32)
    right = np.stack([np.repeat(even.T, 8, axis=1), np.repeat(odd.T, 8, axis=1)]).astype(np.float32)
    return split_host(col), split_host(row), split_host(row_back), jnp.asarray(left), jnp.asarray(right)


def split(value):
    high = value.astype(jnp.bfloat16)
    low = (value - high.astype(jnp.float32)).astype(jnp.bfloat16)
    return high, low


def dot3(a, b, dims=((1,), (0,))):
    def dot(x, y):
        return lax.dot_general(x, y, (dims, ((), ())), preferred_element_type=jnp.float32)

    return dot(a[0], b[0]) + (dot(a[0], b[1]) + dot(a[1], b[0]))


def kernel(
    n_row,
    n_col,
    direction,
    residual,
    weight,
    freq,
    col_h,
    col_l,
    row_h,
    row_l,
    back_h,
    back_l,
    left,
    right,
    applied_out,
    scalars,
    ext,
    res,
    acc,
    own_w,
    got_w,
    spread_w,
    mix,
    red_col,
    red_row,
    part,
    local_sem,
    halo_send,
    halo_recv,
    w_send,
    w_recv,
    col_send,
    col_recv,
    row_send,
    row_recv,
):
    r = lax.axis_index("row")
    c = lax.axis_index("col")
    height, breadth = direction.shape
    win_rows = height // 16
    chunks = breadth // 128 + 1

    fetch_own = pltpu.make_async_copy(direction, ext.at[16 : 16 + height, 128 : 128 + breadth], local_sem.at[0])
    fetch_own.start()
    fetch_res = pltpu.make_async_copy(residual, res, local_sem.at[1])
    fetch_res.start()

    def exists(dr, dc):
        ok = jnp.bool_(True)
        if dr == 1:
            ok = r < n_row - 1
        if dr == -1:
            ok = r > 0
        if dc == 1:
            ok = jnp.logical_and(ok, c < n_col - 1)
        if dc == -1:
            ok = jnp.logical_and(ok, c > 0)
        return ok

    around = [(dr, dc) for dr in (0, -1, 1) for dc in (0, -1, 1) if (dr, dc) != (0, 0)]

    barrier = pltpu.get_barrier_semaphore()
    for k in range(1, n_col):
        pl.semaphore_signal(barrier, inc=1, device_id=(r, lax.rem(c + k, n_col)), device_id_type=MESH)
    for k in range(1, n_row):
        pl.semaphore_signal(barrier, inc=1, device_id=(lax.rem(r + k, n_row), c), device_id_type=MESH)
    for dr, dc in around:
        if dr != 0 and dc != 0:

            @pl.when(exists(dr, dc))
            def _(dr=dr, dc=dc):
                pl.semaphore_signal(barrier, inc=1, device_id=(r + dr, c + dc), device_id_type=MESH)

    vertical = jnp.where(r > 0, 1, 0) + jnp.where(r < n_row - 1, 1, 0)
    horizontal = jnp.where(c > 0, 1, 0) + jnp.where(c < n_col - 1, 1, 0)

    own_w[...] = jnp.zeros_like(own_w)
    own_w[0:win_rows, :] = weight[...]

    pl.semaphore_wait(barrier, n_col - 1 + n_row - 1 + vertical * horizontal)

    src_rows = {0: slice(0, height), -1: slice(0, 16), 1: slice(height - 16, height)}
    src_cols = {0: slice(0, breadth), -1: slice(0, 128), 1: slice(breadth - 128, breadth)}
    dst_rows = {0: slice(16, 16 + height), -1: slice(16 + height, 32 + height), 1: slice(0, 16)}
    dst_cols = {0: slice(128, 128 + breadth), -1: slice(128 + breadth, 256 + breadth), 1: slice(0, 128)}

    def halo(i):
        dr, dc = around[i]
        return pltpu.make_async_remote_copy(
            src_ref=direction.at[src_rows[dr], src_cols[dc]],
            dst_ref=ext.at[dst_rows[dr], dst_cols[dc]],
            send_sem=halo_send.at[i],
            recv_sem=halo_recv.at[i],
            device_id=(r + dr, c + dc),
            device_id_type=MESH,
        )

    forward = [(0, 1), (1, 0), (1, 1)]

    def weights(i):
        dr, dc = forward[i]
        return pltpu.make_async_remote_copy(
            src_ref=own_w,
            dst_ref=got_w.at[i],
            send_sem=w_send.at[i],
            recv_sem=w_recv.at[i],
            device_id=(r + dr, c + dc),
            device_id_type=MESH,
        )

    order = sorted(range(8), key=lambda i: around[i][1] != 0)
    for i in order:

        @pl.when(exists(*around[i]))
        def _(i=i):
            halo(i).start()

    for i in range(3):

        @pl.when(exists(*forward[i]))
        def _(i=i):
            weights(i).start()

    for i, (dr, dc) in enumerate(around):

        @pl.when(jnp.logical_not(exists(-dr, -dc)))
        def _(dr=dr, dc=dc):
            rows, cols = dst_rows[dr], dst_cols[dc]
            ext[rows, cols] = jnp.zeros((rows.stop - rows.start, cols.stop - cols.start), jnp.float32)

    for i, (dr, dc) in enumerate(forward):

        @pl.when(jnp.logical_not(exists(-dr, -dc)))
        def _(i=i):
            got_w[i] = jnp.zeros_like(own_w)

    for m in range(2):
        folded = jnp.dot(left[m], freq[...], precision=lax.Precision.HIGHEST, preferred_element_type=jnp.float32)
        mix[m] = jnp.dot(folded, right[m], precision=lax.Precision.HIGHEST, preferred_element_type=jnp.float32)

    acc[...] = jnp.zeros_like(acc)
    fetch_res.wait()
    fetch_own.wait()

    for i in range(3):
        dr, dc = forward[i]

        @pl.when(exists(-dr, -dc))
        def _(i=i):
            weights(i).wait_recv()

    lane = lax.broadcasted_iota(jnp.int32, (8, 128), 1)
    sub = lax.broadcasted_iota(jnp.int32, (8, 128), 0)

    def stacked(above, here):
        return jnp.where(sub == 0, pltpu.roll(above, 8 - (win_rows - 1), 0), pltpu.roll(here, 1, 0))

    main_w = pltpu.roll(stacked(got_w[1], own_w[...]), 1, 1)
    left_w = pltpu.roll(stacked(got_w[2], got_w[0]), 1, 1)
    shifted = jnp.where(lane == 0, left_w, main_w)
    for k in range(chunks):
        if k == chunks - 1:
            x = jnp.where(lane == 0, main_w, 0.0)
        else:
            x = jnp.where(lane < 8, pltpu.roll(shifted, (128 - 8 * k) % 128, 1) if k else shifted, 0.0)
        for step in (8, 16, 32, 64):
            x = x + pltpu.roll(x, step, 1)
        spread_w[k] = x

    for i in range(8):
        dr, dc = around[i]

        @pl.when(exists(-dr, -dc))
        def _(i=i):
            halo(i).wait_recv()

    even = mix[0]
    odd = mix[1]

    def one_chunk(k):
        start = k * 128 if isinstance(k, int) else pl.multiple_of(k * 128, 128)
        lanes = pl.ds(start, 256)
        col = (col_h[...], col_l[...])
        first = dot3(split(ext[:, lanes]), col)
        coef = dot3((row_h[...], row_l[...]), split(first))
        pieces = []
        for a in range(win_rows + 1):
            z = coef[32 * a : 32 * a + 32]
            swapped = jnp.concatenate([z[16:], z[:16]], axis=0)
            swapped = jnp.concatenate([swapped[:, 128:], swapped[:, :128]], axis=1)
            w = spread_w[k, a : a + 1, :]
            pieces.append((even * z + odd * swapped) * jnp.concatenate([w, w], axis=1))
        weighted = jnp.concatenate(pieces, axis=0)
        rows = dot3((back_h[...], back_l[...]), split(weighted))
        acc[:, lanes] += dot3(split(rows), col, ((1,), (1,)))

    group = 4
    whole_groups = (chunks - 1) // group

    def body(g, carry):
        for k in range(group):
            one_chunk(g * group + k)
        return carry

    lax.fori_loop(0, whole_groups, body, 0)
    for k in range(whole_groups * group, chunks):
        one_chunk(k)

    def sums(k, carry):
        lanes = pl.ds(pl.multiple_of(k * 128, 128), 128)
        inner = pl.ds(pl.multiple_of(k * 128 + 128, 128), 128)
        d = ext[16 : 16 + height, inner]
        e = res[:, lanes]
        q = acc[:, inner] + damping * d
        acc[:, inner] = q
        terms = (e * e, d * q, e * q, q * q)
        return tuple(t + jnp.sum(v.reshape(-1, 8, 128), axis=0) for t, v in zip(carry, terms))

    zero = jnp.zeros((8, 128), jnp.float32)
    totals = lax.fori_loop(0, breadth // 128, sums, (zero,) * 4)
    store = pltpu.make_async_copy(acc.at[:, 128 : 128 + breadth], applied_out, local_sem.at[2])
    store.start()

    tile = jnp.zeros((8, 128), jnp.float32)
    for i, t in enumerate(totals):
        tile = jnp.where(sub == i, jnp.sum(t, axis=0, keepdims=True), tile)

    def exchange(n, me, target, slots, sends, recvs):
        for k in range(1, n):
            to = lax.rem(me + k, n)
            pltpu.make_async_remote_copy(
                src_ref=part,
                dst_ref=slots.at[me],
                send_sem=sends.at[k - 1],
                recv_sem=recvs.at[me],
                device_id=target(to),
                device_id_type=MESH,
            ).start()
        slots[me] = part[...]
        for k in range(1, n):
            source = lax.rem(me + k, n)
            pltpu.make_async_remote_copy(
                src_ref=part,
                dst_ref=slots.at[source],
                send_sem=sends.at[k - 1],
                recv_sem=recvs.at[source],
                device_id=target(source),
                device_id_type=MESH,
            ).wait()
        total = slots[0]
        for k in range(1, n):
            total = total + slots[k]
        return total

    part[...] = tile
    tile = exchange(n_col, c, lambda to: (r, to), red_col, col_send, col_recv)
    part[...] = tile
    tile = exchange(n_row, r, lambda to: (to, c), red_row, row_send, row_recv)

    total = jnp.sum(tile, axis=1, keepdims=True)
    norm_now, curvature, cross, image = (jnp.broadcast_to(total[i : i + 1], (1, 128)) for i in range(4))
    step_length = norm_now / curvature
    norm_next = norm_now - 2.0 * step_length * cross + step_length * step_length * image
    scalars[0:1, :] = step_length
    scalars[1:2, :] = norm_next / norm_now
    scalars[2:8, :] = jnp.zeros((6, 128), jnp.float32)

    for i in range(8):

        @pl.when(exists(*around[i]))
        def _(i=i):
            halo(i).wait_send()

    for i in range(3):

        @pl.when(exists(*forward[i]))
        def _(i=i):
            weights(i).wait_send()

    store.wait()


def per_device(n_row, n_col, iterate, residual, direction, window_weight, freq_weight):
    height, breadth = direction.shape
    win_rows = height // 16
    col, row, back, left, right = host_tables(win_rows)
    vmem = pl.BlockSpec(memory_space=pltpu.VMEM)
    hbm = pl.BlockSpec(memory_space=pl.ANY)
    dma = pltpu.SemaphoreType.DMA
    f32 = jnp.float32
    applied, scalars = pl.pallas_call(
        functools.partial(kernel, n_row, n_col),
        out_shape=(jax.ShapeDtypeStruct((height, breadth), f32), jax.ShapeDtypeStruct((8, 128), f32)),
        in_specs=[hbm, hbm] + [vmem] * 10,
        out_specs=(hbm, vmem),
        scratch_shapes=[
            pltpu.VMEM((height + 32, breadth + 256), f32),
            pltpu.VMEM((height, breadth), f32),
            pltpu.VMEM((height, breadth + 256), f32),
            pltpu.VMEM((8, 128), f32),
            pltpu.VMEM((3, 8, 128), f32),
            pltpu.VMEM((breadth // 128 + 1, 8, 128), f32),
            pltpu.VMEM((2, 32, 256), f32),
            pltpu.VMEM((n_col, 8, 128), f32),
            pltpu.VMEM((n_row, 8, 128), f32),
            pltpu.VMEM((8, 128), f32),
            dma((3,)),
            dma((8,)),
            dma((8,)),
            dma((3,)),
            dma((3,)),
            dma((n_col,)),
            dma((n_col,)),
            dma((n_row,)),
            dma((n_row,)),
        ],
        compiler_params=pltpu.CompilerParams(
            collective_id=0, has_side_effects=True, vmem_limit_bytes=32 * 1024 * 1024
        ),
        cost_estimate=pl.CostEstimate(flops=5_000_000_000, bytes_accessed=2_000_000, transcendentals=0),
    )(direction, residual, window_weight, freq_weight, *col, *row, *back, left, right)
    step_length = scalars[0:1, 0:1]
    ratio = scalars[1:2, 0:1]
    new_iterate = iterate + step_length * direction
    new_residual = residual - step_length * applied
    new_direction = new_residual + ratio * direction
    return (new_iterate, new_residual, new_direction)


def solution(mesh):
    return jax.shard_map(
        functools.partial(per_device, mesh.shape["row"], mesh.shape["col"]),
        mesh=mesh,
        in_specs=(P("row", "col"), P("row", "col"), P("row", "col"), P("row", "col"), P()),
        out_specs=(P("row", "col"), P("row", "col"), P("row", "col")),
        check_vma=False,
    )
```

```python
import functools

import jax
import jax.numpy as jnp
import ml_dtypes
import numpy as np
from jax import lax
from jax.experimental import pallas as pl
from jax.experimental.pallas import tpu as pltpu
from jax.sharding import PartitionSpec as P

MESH = pl.DeviceIdType.MESH
damping = 0.5


def split_host(table, axis):
    table = np.asarray(table, np.float32)
    high = table.astype(ml_dtypes.bfloat16)
    low = (table - high.astype(np.float32)).astype(ml_dtypes.bfloat16)
    return jnp.asarray(np.concatenate([high, high, low], axis=axis).astype(np.float32))


def host_tables(win_rows):
    j = np.arange(32)
    window = np.exp(-0.5 * ((j - 15.5) / 8.0) ** 2)
    basis = np.zeros((2, 16, 32))
    for w in range(16):
        phase = 2.0 * np.pi * w * j / 32.0
        basis[0, w] = np.sqrt(2.0) * np.cos(phase) if w else 1.0
        basis[1, w] = np.sqrt(2.0) * np.sin(phase) if w else (-1.0) ** j
    basis = basis * window / np.sqrt(32.0)
    col = np.zeros((256, 2, 16, 8))
    for b in range(8):
        col[112 + 16 * b : 144 + 16 * b, :, :, b] = basis.transpose(2, 0, 1)
    col = col.reshape(256, 256)
    height = 16 * win_rows
    row = np.zeros((32 * (win_rows + 1), height + 32))
    for a in range(win_rows + 1):
        row[32 * a : 32 * a + 32, 16 * a : 16 * a + 32] = basis.reshape(32, 32)
    row_back = row.T[16 : 16 + height]
    even = np.zeros((2, 16, 32))
    odd = np.zeros((2, 16, 32))
    for h in range(2):
        for w in range(16):
            f = 16 if (h == 1 and w == 0) else w
            even[h, w, f] += 0.5
            even[h, w, -f % 32] += 0.5
            sign = 1.0 - 2.0 * h
            odd[h, w, f] += 0.5 * sign
            odd[h, w, -f % 32] -= 0.5 * sign
    even, odd = even.reshape(32, 32), odd.reshape(32, 32)
    left = np.stack([even, -odd]).astype(np.float32)
    right = np.stack([np.repeat(even.T, 8, axis=1), np.repeat(odd.T, 8, axis=1)]).astype(np.float32)
    tables = (jnp.asarray(col, jnp.float32), jnp.asarray(col.T, jnp.float32))
    tables = tables + (split_host(row, 1), split_host(row_back, 1))
    return tables + (jnp.asarray(left), jnp.asarray(right))


def split(value):
    high = value.astype(jnp.bfloat16)
    low = (value - high.astype(jnp.float32)).astype(jnp.bfloat16)
    return high, low


def thrice(high, low, axis):
    return jnp.concatenate([high, low, high], axis=axis)


def dot(x, y):
    return jnp.dot(x, y, preferred_element_type=jnp.float32)


def kernel(
    n_row,
    n_col,
    direction,
    residual,
    weight_in,
    freq_in,
    col_in,
    col_back_in,
    row_in,
    row_back_in,
    left_in,
    right_in,
    applied_out,
    scalars,
    weight,
    freq,
    col,
    col_back,
    row,
    row_back,
    left,
    right,
    col3,
    col_back3,
    ext,
    res,
    acc,
    first_h,
    first_l,
    own_w,
    got_w,
    spread_w,
    mix,
    red_col,
    red_row,
    part,
    local_sem,
    halo_send,
    halo_recv,
    w_send,
    w_recv,
    col_send,
    col_recv,
    row_send,
    row_recv,
):
    r = lax.axis_index("row")
    c = lax.axis_index("col")
    height, breadth = direction.shape
    win_rows = height // 16
    chunks = breadth // 128 + 1

    places = (
        (weight_in, weight),
        (direction, ext.at[16 : 16 + height, 128 : 128 + breadth]),
        (col_in, col),
        (freq_in, freq),
        (left_in, left),
        (right_in, right),
        (row_in, row),
        (residual, res),
        (row_back_in, row_back),
        (col_back_in, col_back),
    )
    fetches = [pltpu.make_async_copy(a, b, local_sem.at[i]) for i, (a, b) in enumerate(places)]

    def exists(dr, dc):
        ok = jnp.bool_(True)
        if dr == 1:
            ok = r < n_row - 1
        if dr == -1:
            ok = r > 0
        if dc == 1:
            ok = jnp.logical_and(ok, c < n_col - 1)
        if dc == -1:
            ok = jnp.logical_and(ok, c > 0)
        return ok

    around = [(dr, dc) for dr in (0, -1, 1) for dc in (0, -1, 1) if (dr, dc) != (0, 0)]

    barrier = pltpu.get_barrier_semaphore()
    for k in range(1, n_col):
        pl.semaphore_signal(barrier, inc=1, device_id=(r, lax.rem(c + k, n_col)), device_id_type=MESH)
    for k in range(1, n_row):
        pl.semaphore_signal(barrier, inc=1, device_id=(lax.rem(r + k, n_row), c), device_id_type=MESH)
    for dr, dc in around:
        if dr != 0 and dc != 0:

            @pl.when(exists(dr, dc))
            def _(dr=dr, dc=dc):
                pl.semaphore_signal(barrier, inc=1, device_id=(r + dr, c + dc), device_id_type=MESH)

    vertical = jnp.where(r > 0, 1, 0) + jnp.where(r < n_row - 1, 1, 0)
    horizontal = jnp.where(c > 0, 1, 0) + jnp.where(c < n_col - 1, 1, 0)

    for fetch in fetches:
        fetch.start()

    own_w[...] = jnp.zeros_like(own_w)
    fetches[0].wait()
    own_w[0:win_rows, :] = weight[...]

    pl.semaphore_wait(barrier, n_col - 1 + n_row - 1 + vertical * horizontal)

    src_rows = {0: slice(0, height), -1: slice(0, 16), 1: slice(height - 16, height)}
    src_cols = {0: slice(0, breadth), -1: slice(0, 128), 1: slice(breadth - 128, breadth)}
    dst_rows = {0: slice(16, 16 + height), -1: slice(16 + height, 32 + height), 1: slice(0, 16)}
    dst_cols = {0: slice(128, 128 + breadth), -1: slice(128 + breadth, 256 + breadth), 1: slice(0, 128)}

    def halo(i):
        dr, dc = around[i]
        return pltpu.make_async_remote_copy(
            src_ref=direction.at[src_rows[dr], src_cols[dc]],
            dst_ref=ext.at[dst_rows[dr], dst_cols[dc]],
            send_sem=halo_send.at[i],
            recv_sem=halo_recv.at[i],
            device_id=(r + dr, c + dc),
            device_id_type=MESH,
        )

    forward = [(0, 1), (1, 0), (1, 1)]

    def weights(i):
        dr, dc = forward[i]
        return pltpu.make_async_remote_copy(
            src_ref=own_w,
            dst_ref=got_w.at[i],
            send_sem=w_send.at[i],
            recv_sem=w_recv.at[i],
            device_id=(r + dr, c + dc),
            device_id_type=MESH,
        )

    order = sorted(range(8), key=lambda i: around[i][1] != 0)
    for i in order:

        @pl.when(exists(*around[i]))
        def _(i=i):
            halo(i).start()

    for i in range(3):

        @pl.when(exists(*forward[i]))
        def _(i=i):
            weights(i).start()

    for i, (dr, dc) in enumerate(around):

        @pl.when(jnp.logical_not(exists(-dr, -dc)))
        def _(dr=dr, dc=dc):
            rows, cols = dst_rows[dr], dst_cols[dc]
            ext[rows, cols] = jnp.zeros((rows.stop - rows.start, cols.stop - cols.start), jnp.float32)

    for i, (dr, dc) in enumerate(forward):

        @pl.when(jnp.logical_not(exists(-dr, -dc)))
        def _(i=i):
            got_w[i] = jnp.zeros_like(own_w)

    acc[...] = jnp.zeros_like(acc)
    def stack_split(table, stack):
        size = table.shape[0]
        h, l = split(table[...])
        stack[0:size, :] = h
        stack[size : 2 * size, :] = h
        stack[2 * size :, :] = l

    fetches[2].wait()
    stack_split(col, col3)
    fetches[1].wait()

    def columns(regions):
        high, low = [], []
        for k, top, end in regions:
            start = k * 128 if isinstance(k, int) else pl.multiple_of(k * 128, 128)
            h, l = split(ext[top:end, pl.ds(start, 256)])
            high.append(h)
            low.append(l)
        high, low = jnp.concatenate(high, axis=0), jnp.concatenate(low, axis=0)
        h, l = split(dot(thrice(high, low, 1), col3[...]))
        at = 0
        for k, top, end in regions:
            first_h[k, top:end, :] = h[at : at + end - top]
            first_l[k, top:end, :] = l[at : at + end - top]
            at += end - top

    inner = chunks - 2
    group = 5 if inner % 5 == 0 else 1

    def own_columns(g, carry):
        columns([(1 + g * group + k, 16, 16 + height) for k in range(group)])
        return carry

    lax.fori_loop(0, inner // group, own_columns, 0)

    for i in range(3, len(fetches)):
        fetches[i].wait()
    stack_split(col_back, col_back3)
    for m in range(2):
        folded = jnp.dot(left[m], freq[...], precision=lax.Precision.HIGHEST, preferred_element_type=jnp.float32)
        mix[m] = jnp.dot(folded, right[m], precision=lax.Precision.HIGHEST, preferred_element_type=jnp.float32)

    for i in range(3):
        dr, dc = forward[i]

        @pl.when(exists(-dr, -dc))
        def _(i=i):
            weights(i).wait_recv()

    lane = lax.broadcasted_iota(jnp.int32, (8, 128), 1)
    sub = lax.broadcasted_iota(jnp.int32, (8, 128), 0)

    def stacked(above, here):
        return jnp.where(sub == 0, pltpu.roll(above, 8 - (win_rows - 1), 0), pltpu.roll(here, 1, 0))

    main_w = pltpu.roll(stacked(got_w[1], own_w[...]), 1, 1)
    left_w = pltpu.roll(stacked(got_w[2], got_w[0]), 1, 1)
    shifted = jnp.where(lane == 0, left_w, main_w)
    for k in range(chunks):
        if k == chunks - 1:
            x = jnp.where(lane == 0, main_w, 0.0)
        else:
            x = jnp.where(lane < 8, pltpu.roll(shifted, (128 - 8 * k) % 128, 1) if k else shifted, 0.0)
        for step in (8, 16, 32, 64):
            x = x + pltpu.roll(x, step, 1)
        spread_w[k] = x

    for i in range(8):
        dr, dc = around[i]

        @pl.when(exists(-dr, -dc))
        def _(i=i):
            halo(i).wait_recv()

    even = mix[0]
    odd = mix[1]

    rim = [(0, 0, height + 32), (chunks - 1, 0, height + 32)]
    for k in range(1, chunks - 1):
        rim += [(k, 0, 16), (k, 16 + height, 32 + height)]
    columns(rim)

    def rows_of(k):
        coef = dot(row[...].astype(jnp.bfloat16), thrice(first_h[k], first_l[k], 0))
        pieces = []
        for a in range(win_rows + 1):
            z = coef[32 * a : 32 * a + 32]
            swapped = jnp.concatenate([z[16:], z[:16]], axis=0)
            swapped = jnp.concatenate([swapped[:, 128:], swapped[:, :128]], axis=1)
            w = spread_w[k, a : a + 1, :]
            pieces.append((even * z + odd * swapped) * jnp.concatenate([w, w], axis=1))
        h, l = split(jnp.concatenate(pieces, axis=0))
        return split(dot(row_back[...].astype(jnp.bfloat16), thrice(h, l, 0)))

    def chunk_group(ks):
        parts = [rows_of(k) for k in ks]
        h = jnp.concatenate([p[0] for p in parts], axis=0)
        l = jnp.concatenate([p[1] for p in parts], axis=0)
        out = dot(thrice(h, l, 1), col_back3[...])
        for i, k in enumerate(ks):
            start = k * 128 if isinstance(k, int) else pl.multiple_of(k * 128, 128)
            acc[:, pl.ds(start, 256)] += out[i * height : (i + 1) * height]

    def body(g, carry):
        chunk_group([g * group + k for k in range(group)])
        return carry

    lax.fori_loop(0, chunks // group, body, 0)
    if chunks % group:
        chunk_group(list(range(chunks - chunks % group, chunks)))

    def sums(k, carry):
        lanes = pl.ds(pl.multiple_of(k * 128, 128), 128)
        own = pl.ds(pl.multiple_of(k * 128 + 128, 128), 128)
        d = ext[16 : 16 + height, own]
        e = res[:, lanes]
        q = acc[:, own] + damping * d
        acc[:, own] = q
        terms = (e * e, d * q, e * q, q * q)
        return tuple(t + jnp.sum(v.reshape(-1, 8, 128), axis=0) for t, v in zip(carry, terms))

    zero = jnp.zeros((8, 128), jnp.float32)
    totals = lax.fori_loop(0, breadth // 128, sums, (zero,) * 4)
    store = pltpu.make_async_copy(acc.at[:, 128 : 128 + breadth], applied_out, local_sem.at[len(places)])
    store.start()

    tile = jnp.zeros((8, 128), jnp.float32)
    for i, t in enumerate(totals):
        tile = jnp.where(sub == i, jnp.sum(t, axis=0, keepdims=True), tile)

    def exchange(n, me, target, slots, sends, recvs):
        for k in range(1, n):
            to = lax.rem(me + k, n)
            pltpu.make_async_remote_copy(
                src_ref=part,
                dst_ref=slots.at[me],
                send_sem=sends.at[k - 1],
                recv_sem=recvs.at[me],
                device_id=target(to),
                device_id_type=MESH,
            ).start()
        slots[me] = part[...]
        for k in range(1, n):
            source = lax.rem(me + k, n)
            pltpu.make_async_remote_copy(
                src_ref=part,
                dst_ref=slots.at[source],
                send_sem=sends.at[k - 1],
                recv_sem=recvs.at[source],
                device_id=target(source),
                device_id_type=MESH,
            ).wait()
        total = slots[0]
        for k in range(1, n):
            total = total + slots[k]
        return total

    part[...] = tile
    tile = exchange(n_col, c, lambda to: (r, to), red_col, col_send, col_recv)
    part[...] = tile
    tile = exchange(n_row, r, lambda to: (to, c), red_row, row_send, row_recv)

    total = jnp.sum(tile, axis=1, keepdims=True)
    norm_now, curvature, cross, image = (jnp.broadcast_to(total[i : i + 1], (1, 128)) for i in range(4))
    step_length = norm_now / curvature
    norm_next = norm_now - 2.0 * step_length * cross + step_length * step_length * image
    scalars[0:1, :] = step_length
    scalars[1:2, :] = norm_next / norm_now
    scalars[2:8, :] = jnp.zeros((6, 128), jnp.float32)

    for i in range(8):

        @pl.when(exists(*around[i]))
        def _(i=i):
            halo(i).wait_send()

    for i in range(3):

        @pl.when(exists(*forward[i]))
        def _(i=i):
            weights(i).wait_send()

    store.wait()


def update_kernel(scalars, iterate, residual, direction, applied, new_iterate, new_residual, new_direction):
    step_length = scalars[0:1, 0:1]
    ratio = scalars[1:2, 0:1]
    d = direction[...]
    new_iterate[...] = iterate[...] + step_length * d
    rest = residual[...] - step_length * applied[...]
    new_residual[...] = rest
    new_direction[...] = rest + ratio * d


def per_device(n_row, n_col, iterate, residual, direction, window_weight, freq_weight):
    height, breadth = direction.shape
    win_rows = height // 16
    chunks = breadth // 128 + 1
    operands = (direction, residual, window_weight, freq_weight) + host_tables(win_rows)
    vmem = pl.BlockSpec(memory_space=pltpu.VMEM)
    hbm = pl.BlockSpec(memory_space=pl.ANY)
    dma = pltpu.SemaphoreType.DMA
    f32 = jnp.float32
    applied, scalars = pl.pallas_call(
        functools.partial(kernel, n_row, n_col),
        out_shape=(jax.ShapeDtypeStruct((height, breadth), f32), jax.ShapeDtypeStruct((8, 128), f32)),
        in_specs=[hbm] * len(operands),
        out_specs=(hbm, vmem),
        scratch_shapes=[pltpu.VMEM(x.shape, x.dtype) for x in operands[2:]]
        + [
            pltpu.VMEM((768, 256), jnp.bfloat16),
            pltpu.VMEM((768, 256), jnp.bfloat16),
            pltpu.VMEM((height + 32, breadth + 256), f32),
            pltpu.VMEM((height, breadth), f32),
            pltpu.VMEM((height, breadth + 256), f32),
            pltpu.VMEM((chunks, height + 32, 256), jnp.bfloat16),
            pltpu.VMEM((chunks, height + 32, 256), jnp.bfloat16),
            pltpu.VMEM((8, 128), f32),
            pltpu.VMEM((3, 8, 128), f32),
            pltpu.VMEM((chunks, 8, 128), f32),
            pltpu.VMEM((2, 32, 256), f32),
            pltpu.VMEM((n_col, 8, 128), f32),
            pltpu.VMEM((n_row, 8, 128), f32),
            pltpu.VMEM((8, 128), f32),
            dma((len(operands) + 1,)),
            dma((8,)),
            dma((8,)),
            dma((3,)),
            dma((3,)),
            dma((n_col,)),
            dma((n_col,)),
            dma((n_row,)),
            dma((n_row,)),
        ],
        compiler_params=pltpu.CompilerParams(
            collective_id=0, has_side_effects=True, vmem_limit_bytes=60 * 1024 * 1024
        ),
        cost_estimate=pl.CostEstimate(flops=5_000_000_000, bytes_accessed=2_000_000, transcendentals=0),
    )(*operands)
    block = pl.BlockSpec((height, 512), lambda i: (0, i))
    return pl.pallas_call(
        update_kernel,
        grid=(breadth // 512,),
        out_shape=(jax.ShapeDtypeStruct((height, breadth), f32),) * 3,
        in_specs=[pl.BlockSpec((8, 128), lambda i: (0, 0))] + [block] * 4,
        out_specs=(block,) * 3,
        compiler_params=pltpu.CompilerParams(vmem_limit_bytes=60 * 1024 * 1024),
    )(scalars, iterate, residual, direction, applied)


def solution(mesh):
    return jax.shard_map(
        functools.partial(per_device, mesh.shape["row"], mesh.shape["col"]),
        mesh=mesh,
        in_specs=(P("row", "col"), P("row", "col"), P("row", "col"), P("row", "col"), P()),
        out_specs=(P("row", "col"), P("row", "col"), P("row", "col")),
        check_vma=False,
    )
```

```python
import functools

import jax
import jax.numpy as jnp
import ml_dtypes
import numpy as np
from jax import lax
from jax.experimental import pallas as pl
from jax.experimental.pallas import tpu as pltpu
from jax.sharding import PartitionSpec as P

MESH = pl.DeviceIdType.MESH
damping = 0.5


def split_host(table, axis):
    table = np.asarray(table, np.float32)
    high = table.astype(ml_dtypes.bfloat16)
    low = (table - high.astype(np.float32)).astype(ml_dtypes.bfloat16)
    return jnp.asarray(np.concatenate([high, high, low], axis=axis).astype(np.float32))


def host_tables(win_rows):
    j = np.arange(32)
    window = np.exp(-0.5 * ((j - 15.5) / 8.0) ** 2)
    basis = np.zeros((2, 16, 32))
    for w in range(16):
        phase = 2.0 * np.pi * w * j / 32.0
        basis[0, w] = np.sqrt(2.0) * np.cos(phase) if w else 1.0
        basis[1, w] = np.sqrt(2.0) * np.sin(phase) if w else (-1.0) ** j
    basis = basis * window / np.sqrt(32.0)
    col = np.zeros((256, 2, 16, 8))
    for b in range(8):
        col[112 + 16 * b : 144 + 16 * b, :, :, b] = basis.transpose(2, 0, 1)
    col = col.reshape(256, 256)
    height = 16 * win_rows
    row = np.zeros((32 * (win_rows + 1), height + 32))
    for a in range(win_rows + 1):
        row[32 * a : 32 * a + 32, 16 * a : 16 * a + 32] = basis.reshape(32, 32)
    row_back = row.T[16 : 16 + height]
    even = np.zeros((2, 16, 32))
    odd = np.zeros((2, 16, 32))
    for h in range(2):
        for w in range(16):
            f = 16 if (h == 1 and w == 0) else w
            even[h, w, f] += 0.5
            even[h, w, -f % 32] += 0.5
            sign = 1.0 - 2.0 * h
            odd[h, w, f] += 0.5 * sign
            odd[h, w, -f % 32] -= 0.5 * sign
    even, odd = even.reshape(32, 32), odd.reshape(32, 32)
    left = np.stack([even, -odd]).astype(np.float32)
    right = np.stack([np.repeat(even.T, 8, axis=1), np.repeat(odd.T, 8, axis=1)]).astype(np.float32)
    tables = (jnp.asarray(col, jnp.float32), jnp.asarray(col.T, jnp.float32))
    rim = np.r_[0:32, height : height + 32]
    rim_windows = np.r_[0:32, 32 * win_rows : 32 * win_rows + 32]
    inside = row[32 : 32 * win_rows, 16 : 16 + height]
    tables = tables + (split_host(inside, 1), split_host(row[rim_windows][:, rim], 1), split_host(row_back, 1))
    return tables + (jnp.asarray(left), jnp.asarray(right))


def split(value):
    high = value.astype(jnp.bfloat16)
    low = (value - high.astype(jnp.float32)).astype(jnp.bfloat16)
    return high, low


def thrice(high, low, axis):
    return jnp.concatenate([high, low, high], axis=axis)


def dot(x, y):
    return jnp.dot(x, y, preferred_element_type=jnp.float32)


def kernel(
    n_row,
    n_col,
    direction,
    residual,
    weight_in,
    freq_in,
    col_in,
    col_back_in,
    row_in,
    row_rim_in,
    row_back_in,
    left_in,
    right_in,
    applied_out,
    scalars,
    weight,
    freq,
    col,
    col_back,
    row,
    row_rim,
    row_back,
    left,
    right,
    col3,
    col_back3,
    ext,
    res,
    acc,
    first_h,
    first_l,
    mid_h,
    mid_l,
    row_b,
    row_rim_b,
    row_back_b,
    own_w,
    got_w,
    spread_w,
    mix,
    red_col,
    red_row,
    part,
    local_sem,
    halo_send,
    halo_recv,
    w_send,
    w_recv,
    col_send,
    col_recv,
    row_send,
    row_recv,
):
    r = lax.axis_index("row")
    c = lax.axis_index("col")
    height, breadth = direction.shape
    win_rows = height // 16
    chunks = breadth // 128 + 1

    places = (
        (weight_in, weight),
        (direction, ext.at[16 : 16 + height, 128 : 128 + breadth]),
        (col_in, col),
        (freq_in, freq),
        (left_in, left),
        (right_in, right),
        (row_in, row),
        (row_rim_in, row_rim),
        (residual, res),
        (row_back_in, row_back),
        (col_back_in, col_back),
    )
    fetches = [pltpu.make_async_copy(a, b, local_sem.at[i]) for i, (a, b) in enumerate(places)]

    def exists(dr, dc):
        ok = jnp.bool_(True)
        if dr == 1:
            ok = r < n_row - 1
        if dr == -1:
            ok = r > 0
        if dc == 1:
            ok = jnp.logical_and(ok, c < n_col - 1)
        if dc == -1:
            ok = jnp.logical_and(ok, c > 0)
        return ok

    around = [(dr, dc) for dr in (0, -1, 1) for dc in (0, -1, 1) if (dr, dc) != (0, 0)]

    barrier = pltpu.get_barrier_semaphore()
    for k in range(1, n_col):
        pl.semaphore_signal(barrier, inc=1, device_id=(r, lax.rem(c + k, n_col)), device_id_type=MESH)
    for k in range(1, n_row):
        pl.semaphore_signal(barrier, inc=1, device_id=(lax.rem(r + k, n_row), c), device_id_type=MESH)
    for dr, dc in around:
        if dr != 0 and dc != 0:

            @pl.when(exists(dr, dc))
            def _(dr=dr, dc=dc):
                pl.semaphore_signal(barrier, inc=1, device_id=(r + dr, c + dc), device_id_type=MESH)

    vertical = jnp.where(r > 0, 1, 0) + jnp.where(r < n_row - 1, 1, 0)
    horizontal = jnp.where(c > 0, 1, 0) + jnp.where(c < n_col - 1, 1, 0)

    for fetch in fetches:
        fetch.start()

    own_w[...] = jnp.zeros_like(own_w)
    fetches[0].wait()
    own_w[0:win_rows, :] = weight[...]

    pl.semaphore_wait(barrier, n_col - 1 + n_row - 1 + vertical * horizontal)

    src_rows = {0: slice(0, height), -1: slice(0, 16), 1: slice(height - 16, height)}
    src_cols = {0: slice(0, breadth), -1: slice(0, 128), 1: slice(breadth - 128, breadth)}
    dst_rows = {0: slice(16, 16 + height), -1: slice(16 + height, 32 + height), 1: slice(0, 16)}
    dst_cols = {0: slice(128, 128 + breadth), -1: slice(128 + breadth, 256 + breadth), 1: slice(0, 128)}

    def halo(i):
        dr, dc = around[i]
        return pltpu.make_async_remote_copy(
            src_ref=direction.at[src_rows[dr], src_cols[dc]],
            dst_ref=ext.at[dst_rows[dr], dst_cols[dc]],
            send_sem=halo_send.at[i],
            recv_sem=halo_recv.at[i],
            device_id=(r + dr, c + dc),
            device_id_type=MESH,
        )

    forward = [(0, 1), (1, 0), (1, 1)]

    def weights(i):
        dr, dc = forward[i]
        return pltpu.make_async_remote_copy(
            src_ref=own_w,
            dst_ref=got_w.at[i],
            send_sem=w_send.at[i],
            recv_sem=w_recv.at[i],
            device_id=(r + dr, c + dc),
            device_id_type=MESH,
        )

    for i in range(3):

        @pl.when(exists(*forward[i]))
        def _(i=i):
            weights(i).start()

    order = sorted(range(8), key=lambda i: around[i][1] != 0)
    for i in order:

        @pl.when(exists(*around[i]))
        def _(i=i):
            halo(i).start()

    for i, (dr, dc) in enumerate(around):

        @pl.when(jnp.logical_not(exists(-dr, -dc)))
        def _(dr=dr, dc=dc):
            rows, cols = dst_rows[dr], dst_cols[dc]
            ext[rows, cols] = jnp.zeros((rows.stop - rows.start, cols.stop - cols.start), jnp.float32)

    for i, (dr, dc) in enumerate(forward):

        @pl.when(jnp.logical_not(exists(-dr, -dc)))
        def _(i=i):
            got_w[i] = jnp.zeros_like(own_w)

    acc[...] = jnp.zeros_like(acc)
    def stack_split(table, stack):
        size = table.shape[0]
        h, l = split(table[...])
        stack[0:size, :] = h
        stack[size : 2 * size, :] = h
        stack[2 * size :, :] = l

    fetches[2].wait()
    stack_split(col, col3)
    fetches[1].wait()

    def columns(regions):
        high, low = [], []
        for k, top, end in regions:
            start = k * 128 if isinstance(k, int) else pl.multiple_of(k * 128, 128)
            h, l = split(ext[top:end, pl.ds(start, 256)])
            high.append(h)
            low.append(l)
        high, low = jnp.concatenate(high, axis=0), jnp.concatenate(low, axis=0)
        h, l = split(dot(thrice(high, low, 1), col3[...]))
        at = 0
        for k, top, end in regions:
            first_h[k, top:end, :] = h[at : at + end - top]
            first_l[k, top:end, :] = l[at : at + end - top]
            at += end - top

    for i in range(3, len(fetches)):
        fetches[i].wait()
    stack_split(col_back, col_back3)
    for table, cast in ((row, row_b), (row_rim, row_rim_b), (row_back, row_back_b)):
        cast[...] = table[...].astype(jnp.bfloat16)
    for m in range(2):
        folded = jnp.dot(left[m], freq[...], precision=lax.Precision.HIGHEST, preferred_element_type=jnp.float32)
        mix[m] = jnp.dot(folded, right[m], precision=lax.Precision.HIGHEST, preferred_element_type=jnp.float32)

    for i in range(3):
        dr, dc = forward[i]

        @pl.when(exists(-dr, -dc))
        def _(i=i):
            weights(i).wait_recv()

    lane = lax.broadcasted_iota(jnp.int32, (8, 128), 1)
    sub = lax.broadcasted_iota(jnp.int32, (8, 128), 0)

    def stacked(above, here):
        return jnp.where(sub == 0, pltpu.roll(above, 8 - (win_rows - 1), 0), pltpu.roll(here, 1, 0))

    main_w = pltpu.roll(stacked(got_w[1], own_w[...]), 1, 1)
    left_w = pltpu.roll(stacked(got_w[2], got_w[0]), 1, 1)
    shifted = jnp.where(lane == 0, left_w, main_w)
    for k in range(chunks):
        if k == chunks - 1:
            x = jnp.where(lane == 0, main_w, 0.0)
        else:
            x = jnp.where(lane < 8, pltpu.roll(shifted, (128 - 8 * k) % 128, 1) if k else shifted, 0.0)
        for step in (8, 16, 32, 64):
            x = x + pltpu.roll(x, step, 1)
        spread_w[k] = x

    even = mix[0]
    odd = mix[1]

    def weigh(coef, k, windows):
        pieces = []
        for i, a in enumerate(windows):
            z = coef[32 * i : 32 * i + 32]
            swapped = jnp.concatenate([z[16:], z[:16]], axis=0)
            swapped = jnp.concatenate([swapped[:, 128:], swapped[:, :128]], axis=1)
            w = spread_w[k, a : a + 1, :]
            pieces.append((even * z + odd * swapped) * jnp.concatenate([w, w], axis=1))
        return split(jnp.concatenate(pieces, axis=0))

    def inside_windows(k):
        coef = dot(row_b[...], thrice(first_h[k, 16 : 16 + height], first_l[k, 16 : 16 + height], 0))
        h, l = weigh(coef, k, range(1, win_rows))
        mid_h[k] = h
        mid_l[k] = l

    inner = chunks - 2
    group = 5 if inner % 5 == 0 else 1

    def own_columns(g, carry):
        ks = [1 + g * group + k for k in range(group)]
        columns([(k, 16, 16 + height) for k in ks])
        for k in ks:
            inside_windows(k)
        return carry

    lax.fori_loop(0, inner // group, own_columns, 0)

    for i in range(8):
        dr, dc = around[i]

        @pl.when(exists(-dr, -dc))
        def _(i=i):
            halo(i).wait_recv()

    rim = [(0, 0, height + 32), (chunks - 1, 0, height + 32)]
    for k in range(1, chunks - 1):
        rim += [(k, 0, 16), (k, 16 + height, 32 + height)]
    columns(rim)
    inside_windows(0)
    inside_windows(chunks - 1)

    def rows_of(k):
        h, l = (jnp.concatenate([x[k, 0:32], x[k, height : height + 32]], axis=0) for x in (first_h, first_l))
        coef = dot(row_rim_b[...], thrice(h, l, 0))
        h, l = weigh(coef, k, (0, win_rows))
        h = jnp.concatenate([h[:32], mid_h[k], h[32:]], axis=0)
        l = jnp.concatenate([l[:32], mid_l[k], l[32:]], axis=0)
        return split(dot(row_back_b[...], thrice(h, l, 0)))

    def chunk_group(ks):
        parts = [rows_of(k) for k in ks]
        h = jnp.concatenate([p[0] for p in parts], axis=0)
        l = jnp.concatenate([p[1] for p in parts], axis=0)
        out = dot(thrice(h, l, 1), col_back3[...])
        for i, k in enumerate(ks):
            start = k * 128 if isinstance(k, int) else pl.multiple_of(k * 128, 128)
            acc[:, pl.ds(start, 256)] += out[i * height : (i + 1) * height]

    def body(g, carry):
        chunk_group([g * group + k for k in range(group)])
        return carry

    lax.fori_loop(0, chunks // group, body, 0)
    if chunks % group:
        chunk_group(list(range(chunks - chunks % group, chunks)))

    def sums(k, carry):
        lanes = pl.ds(pl.multiple_of(k * 128, 128), 128)
        own = pl.ds(pl.multiple_of(k * 128 + 128, 128), 128)
        d = ext[16 : 16 + height, own]
        e = res[:, lanes]
        q = acc[:, own] + damping * d
        acc[:, own] = q
        terms = (e * e, d * q, e * q, q * q)
        return tuple(t + jnp.sum(v.reshape(-1, 8, 128), axis=0) for t, v in zip(carry, terms))

    zero = jnp.zeros((8, 128), jnp.float32)
    totals = lax.fori_loop(0, breadth // 128, sums, (zero,) * 4)
    store = pltpu.make_async_copy(acc.at[:, 128 : 128 + breadth], applied_out, local_sem.at[len(places)])
    store.start()

    tile = jnp.zeros((8, 128), jnp.float32)
    for i, t in enumerate(totals):
        tile = jnp.where(sub == i, jnp.sum(t, axis=0, keepdims=True), tile)

    def exchange(n, me, target, slots, sends, recvs):
        for k in range(1, n):
            to = lax.rem(me + k, n)
            pltpu.make_async_remote_copy(
                src_ref=part,
                dst_ref=slots.at[me],
                send_sem=sends.at[k - 1],
                recv_sem=recvs.at[me],
                device_id=target(to),
                device_id_type=MESH,
            ).start()
        slots[me] = part[...]
        for k in range(1, n):
            source = lax.rem(me + k, n)
            pltpu.make_async_remote_copy(
                src_ref=part,
                dst_ref=slots.at[source],
                send_sem=sends.at[k - 1],
                recv_sem=recvs.at[source],
                device_id=target(source),
                device_id_type=MESH,
            ).wait()
        total = slots[0]
        for k in range(1, n):
            total = total + slots[k]
        return total

    part[...] = tile
    tile = exchange(n_col, c, lambda to: (r, to), red_col, col_send, col_recv)
    part[...] = tile
    tile = exchange(n_row, r, lambda to: (to, c), red_row, row_send, row_recv)

    total = jnp.sum(tile, axis=1, keepdims=True)
    norm_now, curvature, cross, image = (jnp.broadcast_to(total[i : i + 1], (1, 128)) for i in range(4))
    step_length = norm_now / curvature
    norm_next = norm_now - 2.0 * step_length * cross + step_length * step_length * image
    scalars[0:1, :] = step_length
    scalars[1:2, :] = norm_next / norm_now
    scalars[2:8, :] = jnp.zeros((6, 128), jnp.float32)

    for i in range(8):

        @pl.when(exists(*around[i]))
        def _(i=i):
            halo(i).wait_send()

    for i in range(3):

        @pl.when(exists(*forward[i]))
        def _(i=i):
            weights(i).wait_send()

    store.wait()


def update_kernel(
    scalars, iterate, residual, direction, applied, new_iterate, new_residual, new_direction, held, made, sem_in, sem_out
):
    parts = 4
    rows = iterate.shape[0] // parts
    fetches, stores = [], []
    for p in range(parts):
        here = pl.ds(p * rows, rows)
        for i, x in enumerate((direction, iterate, residual, applied)):
            fetches.append(pltpu.make_async_copy(x.at[here], held.at[i, here], sem_in.at[p, i]))
        for i, x in enumerate((new_iterate, new_residual, new_direction)):
            stores.append(pltpu.make_async_copy(made.at[i, here], x.at[here], sem_out.at[p, i]))
    for fetch in fetches:
        fetch.start()
    step_length = scalars[0:1, 0:1]
    ratio = scalars[1:2, 0:1]
    for p in range(parts):
        here = pl.ds(p * rows, rows)
        for fetch in fetches[4 * p : 4 * p + 4]:
            fetch.wait()
        d = held[0, here]
        made[0, here] = held[1, here] + step_length * d
        rest = held[2, here] - step_length * held[3, here]
        made[1, here] = rest
        made[2, here] = rest + ratio * d
        for store in stores[3 * p : 3 * p + 3]:
            store.start()
    for store in stores:
        store.wait()


def per_device(n_row, n_col, iterate, residual, direction, window_weight, freq_weight):
    height, breadth = direction.shape
    win_rows = height // 16
    chunks = breadth // 128 + 1
    operands = (direction, residual, window_weight, freq_weight) + host_tables(win_rows)
    vmem = pl.BlockSpec(memory_space=pltpu.VMEM)
    hbm = pl.BlockSpec(memory_space=pl.ANY)
    dma = pltpu.SemaphoreType.DMA
    f32 = jnp.float32
    applied, scalars = pl.pallas_call(
        functools.partial(kernel, n_row, n_col),
        out_shape=(jax.ShapeDtypeStruct((height, breadth), f32), jax.ShapeDtypeStruct((8, 128), f32)),
        in_specs=[hbm] * len(operands),
        out_specs=(hbm, vmem),
        scratch_shapes=[pltpu.VMEM(x.shape, x.dtype) for x in operands[2:]]
        + [
            pltpu.VMEM((768, 256), jnp.bfloat16),
            pltpu.VMEM((768, 256), jnp.bfloat16),
            pltpu.VMEM((height + 32, breadth + 256), f32),
            pltpu.VMEM((height, breadth), f32),
            pltpu.VMEM((height, breadth + 256), f32),
            pltpu.VMEM((chunks, height + 32, 256), jnp.bfloat16),
            pltpu.VMEM((chunks, height + 32, 256), jnp.bfloat16),
            pltpu.VMEM((chunks, 32 * (win_rows - 1), 256), jnp.bfloat16),
            pltpu.VMEM((chunks, 32 * (win_rows - 1), 256), jnp.bfloat16),
        ]
        + [pltpu.VMEM(x.shape, jnp.bfloat16) for x in operands[6:9]]
        + [
            pltpu.VMEM((8, 128), f32),
            pltpu.VMEM((3, 8, 128), f32),
            pltpu.VMEM((chunks, 8, 128), f32),
            pltpu.VMEM((2, 32, 256), f32),
            pltpu.VMEM((n_col, 8, 128), f32),
            pltpu.VMEM((n_row, 8, 128), f32),
            pltpu.VMEM((8, 128), f32),
            dma((len(operands) + 1,)),
            dma((8,)),
            dma((8,)),
            dma((3,)),
            dma((3,)),
            dma((n_col,)),
            dma((n_col,)),
            dma((n_row,)),
            dma((n_row,)),
        ],
        compiler_params=pltpu.CompilerParams(
            collective_id=0, has_side_effects=True, vmem_limit_bytes=60 * 1024 * 1024
        ),
        cost_estimate=pl.CostEstimate(flops=5_000_000_000, bytes_accessed=2_000_000, transcendentals=0),
    )(*operands)
    return pl.pallas_call(
        update_kernel,
        out_shape=(jax.ShapeDtypeStruct((height, breadth), f32),) * 3,
        in_specs=[vmem] + [hbm] * 4,
        out_specs=(hbm,) * 3,
        scratch_shapes=[
            pltpu.VMEM((4, height, breadth), f32),
            pltpu.VMEM((3, height, breadth), f32),
            dma((4, 4)),
            dma((4, 3)),
        ],
        compiler_params=pltpu.CompilerParams(vmem_limit_bytes=60 * 1024 * 1024),
    )(scalars, iterate, residual, direction, applied)


def solution(mesh):
    return jax.shard_map(
        functools.partial(per_device, mesh.shape["row"], mesh.shape["col"]),
        mesh=mesh,
        in_specs=(P("row", "col"), P("row", "col"), P("row", "col"), P("row", "col"), P()),
        out_specs=(P("row", "col"), P("row", "col"), P("row", "col")),
        check_vma=False,
    )
```

```python
import functools

import jax
import jax.numpy as jnp
import ml_dtypes
import numpy as np
from jax import lax
from jax.experimental import pallas as pl
from jax.experimental.pallas import tpu as pltpu
from jax.sharding import PartitionSpec as P

MESH = pl.DeviceIdType.MESH
damping = 0.5


def split_host(table, axis):
    table = np.asarray(table, np.float32)
    high = table.astype(ml_dtypes.bfloat16)
    low = (table - high.astype(np.float32)).astype(ml_dtypes.bfloat16)
    return jnp.asarray(np.concatenate([high, high, low], axis=axis).astype(np.float32))


def host_tables(win_rows):
    j = np.arange(32)
    window = np.exp(-0.5 * ((j - 15.5) / 8.0) ** 2)
    basis = np.zeros((2, 16, 32))
    for w in range(16):
        phase = 2.0 * np.pi * w * j / 32.0
        basis[0, w] = np.sqrt(2.0) * np.cos(phase) if w else 1.0
        basis[1, w] = np.sqrt(2.0) * np.sin(phase) if w else (-1.0) ** j
    basis = basis * window / np.sqrt(32.0)
    col = np.zeros((256, 2, 16, 8))
    for b in range(8):
        col[112 + 16 * b : 144 + 16 * b, :, :, b] = basis.transpose(2, 0, 1)
    col = col.reshape(256, 256)
    height = 16 * win_rows
    row = np.zeros((32 * (win_rows + 1), height + 32))
    for a in range(win_rows + 1):
        row[32 * a : 32 * a + 32, 16 * a : 16 * a + 32] = basis.reshape(32, 32)
    row_back = row.T[16 : 16 + height]
    even = np.zeros((2, 16, 32))
    odd = np.zeros((2, 16, 32))
    for h in range(2):
        for w in range(16):
            f = 16 if (h == 1 and w == 0) else w
            even[h, w, f] += 0.5
            even[h, w, -f % 32] += 0.5
            sign = 1.0 - 2.0 * h
            odd[h, w, f] += 0.5 * sign
            odd[h, w, -f % 32] -= 0.5 * sign
    even, odd = even.reshape(32, 32), odd.reshape(32, 32)
    left = np.stack([even, -odd]).astype(np.float32)
    right = np.stack([np.repeat(even.T, 8, axis=1), np.repeat(odd.T, 8, axis=1)]).astype(np.float32)
    tables = (jnp.asarray(col, jnp.float32), jnp.asarray(col.T, jnp.float32))
    rim = np.r_[0:32, height : height + 32]
    rim_windows = np.r_[0:32, 32 * win_rows : 32 * win_rows + 32]
    inside = row[32 : 32 * win_rows, 16 : 16 + height]
    tables = tables + (split_host(inside, 1), split_host(row[rim_windows][:, rim], 1), split_host(row_back, 1))
    return tables + (jnp.asarray(left), jnp.asarray(right))


def split(value):
    high = value.astype(jnp.bfloat16)
    low = (value - high.astype(jnp.float32)).astype(jnp.bfloat16)
    return high, low


def thrice(high, low, axis):
    return jnp.concatenate([high, low, high], axis=axis)


def dot(x, y):
    return jnp.dot(x, y, preferred_element_type=jnp.float32)


def kernel(
    n_row,
    n_col,
    direction,
    residual,
    weight_in,
    freq_in,
    col_in,
    col_back_in,
    row_in,
    row_rim_in,
    row_back_in,
    left_in,
    right_in,
    applied_out,
    scalars,
    weight,
    freq,
    col,
    col_back,
    row,
    row_rim,
    row_back,
    left,
    right,
    col3,
    col_back3,
    ext,
    res,
    acc,
    first_h,
    first_l,
    mid_h,
    mid_l,
    row_b,
    row_rim_b,
    row_back_b,
    own_w,
    got_w,
    spread_w,
    mix,
    red_col,
    red_row,
    part,
    local_sem,
    halo_send,
    halo_recv,
    w_send,
    w_recv,
    col_send,
    col_recv,
    row_send,
    row_recv,
):
    r = lax.axis_index("row")
    c = lax.axis_index("col")
    height, breadth = direction.shape
    win_rows = height // 16
    chunks = breadth // 128 + 1

    places = (
        (weight_in, weight),
        (direction, ext.at[16 : 16 + height, 128 : 128 + breadth]),
        (col_in, col),
        (freq_in, freq),
        (left_in, left),
        (right_in, right),
        (row_in, row),
        (row_rim_in, row_rim),
        (residual, res),
        (row_back_in, row_back),
        (col_back_in, col_back),
    )
    fetches = [pltpu.make_async_copy(a, b, local_sem.at[i]) for i, (a, b) in enumerate(places)]

    def exists(dr, dc):
        ok = jnp.bool_(True)
        if dr == 1:
            ok = r < n_row - 1
        if dr == -1:
            ok = r > 0
        if dc == 1:
            ok = jnp.logical_and(ok, c < n_col - 1)
        if dc == -1:
            ok = jnp.logical_and(ok, c > 0)
        return ok

    around = [(dr, dc) for dr in (0, -1, 1) for dc in (0, -1, 1) if (dr, dc) != (0, 0)]

    barrier = pltpu.get_barrier_semaphore()
    for k in range(1, n_col):
        pl.semaphore_signal(barrier, inc=1, device_id=(r, lax.rem(c + k, n_col)), device_id_type=MESH)
    for k in range(1, n_row):
        pl.semaphore_signal(barrier, inc=1, device_id=(lax.rem(r + k, n_row), c), device_id_type=MESH)
    for dr, dc in around:
        if dr != 0 and dc != 0:

            @pl.when(exists(dr, dc))
            def _(dr=dr, dc=dc):
                pl.semaphore_signal(barrier, inc=1, device_id=(r + dr, c + dc), device_id_type=MESH)

    vertical = jnp.where(r > 0, 1, 0) + jnp.where(r < n_row - 1, 1, 0)
    horizontal = jnp.where(c > 0, 1, 0) + jnp.where(c < n_col - 1, 1, 0)

    for fetch in fetches:
        fetch.start()

    own_w[...] = jnp.zeros_like(own_w)
    fetches[0].wait()
    own_w[0:win_rows, :] = weight[...]

    pl.semaphore_wait(barrier, n_col - 1 + n_row - 1 + vertical * horizontal)

    src_rows = {0: slice(0, height), -1: slice(0, 16), 1: slice(height - 16, height)}
    src_cols = {0: slice(0, breadth), -1: slice(0, 128), 1: slice(breadth - 128, breadth)}
    dst_rows = {0: slice(16, 16 + height), -1: slice(16 + height, 32 + height), 1: slice(0, 16)}
    dst_cols = {0: slice(128, 128 + breadth), -1: slice(128 + breadth, 256 + breadth), 1: slice(0, 128)}

    def halo(i):
        dr, dc = around[i]
        return pltpu.make_async_remote_copy(
            src_ref=direction.at[src_rows[dr], src_cols[dc]],
            dst_ref=ext.at[dst_rows[dr], dst_cols[dc]],
            send_sem=halo_send.at[i],
            recv_sem=halo_recv.at[i],
            device_id=(r + dr, c + dc),
            device_id_type=MESH,
        )

    forward = [(0, 1), (1, 0), (1, 1)]

    def weights(i):
        dr, dc = forward[i]
        return pltpu.make_async_remote_copy(
            src_ref=own_w,
            dst_ref=got_w.at[i],
            send_sem=w_send.at[i],
            recv_sem=w_recv.at[i],
            device_id=(r + dr, c + dc),
            device_id_type=MESH,
        )

    for i in range(3):

        @pl.when(exists(*forward[i]))
        def _(i=i):
            weights(i).start()

    order = sorted(range(8), key=lambda i: around[i][1] != 0)
    for i in order:

        @pl.when(exists(*around[i]))
        def _(i=i):
            halo(i).start()

    for i, (dr, dc) in enumerate(around):

        @pl.when(jnp.logical_not(exists(-dr, -dc)))
        def _(dr=dr, dc=dc):
            rows, cols = dst_rows[dr], dst_cols[dc]
            ext[rows, cols] = jnp.zeros((rows.stop - rows.start, cols.stop - cols.start), jnp.float32)

    for i, (dr, dc) in enumerate(forward):

        @pl.when(jnp.logical_not(exists(-dr, -dc)))
        def _(i=i):
            got_w[i] = jnp.zeros_like(own_w)

    acc[...] = jnp.zeros_like(acc)
    def stack_split(table, stack):
        size = table.shape[0]
        h, l = split(table[...])
        stack[0:size, :] = h
        stack[size : 2 * size, :] = h
        stack[2 * size :, :] = l

    fetches[2].wait()
    stack_split(col, col3)
    fetches[1].wait()

    def columns(regions):
        high, low = [], []
        for k, top, end in regions:
            start = k * 128 if isinstance(k, int) else pl.multiple_of(k * 128, 128)
            h, l = split(ext[top:end, pl.ds(start, 256)])
            high.append(h)
            low.append(l)
        high, low = jnp.concatenate(high, axis=0), jnp.concatenate(low, axis=0)
        h, l = split(dot(thrice(high, low, 1), col3[...]))
        at = 0
        for k, top, end in regions:
            first_h[k, top:end, :] = h[at : at + end - top]
            first_l[k, top:end, :] = l[at : at + end - top]
            at += end - top

    for i in range(3, len(fetches)):
        fetches[i].wait()
    stack_split(col_back, col_back3)
    for table, cast in ((row, row_b), (row_rim, row_rim_b), (row_back, row_back_b)):
        cast[...] = table[...].astype(jnp.bfloat16)
    for m in range(2):
        folded = jnp.dot(left[m], freq[...], precision=lax.Precision.HIGHEST, preferred_element_type=jnp.float32)
        mix[m] = jnp.dot(folded, right[m], precision=lax.Precision.HIGHEST, preferred_element_type=jnp.float32)

    for i in range(3):
        dr, dc = forward[i]

        @pl.when(exists(-dr, -dc))
        def _(i=i):
            weights(i).wait_recv()

    lane = lax.broadcasted_iota(jnp.int32, (8, 128), 1)
    sub = lax.broadcasted_iota(jnp.int32, (8, 128), 0)

    def stacked(above, here):
        return jnp.where(sub == 0, pltpu.roll(above, 8 - (win_rows - 1), 0), pltpu.roll(here, 1, 0))

    main_w = pltpu.roll(stacked(got_w[1], own_w[...]), 1, 1)
    left_w = pltpu.roll(stacked(got_w[2], got_w[0]), 1, 1)
    shifted = jnp.where(lane == 0, left_w, main_w)
    for k in range(chunks):
        if k == chunks - 1:
            x = jnp.where(lane == 0, main_w, 0.0)
        else:
            x = jnp.where(lane < 8, pltpu.roll(shifted, (128 - 8 * k) % 128, 1) if k else shifted, 0.0)
        for step in (8, 16, 32, 64):
            x = x + pltpu.roll(x, step, 1)
        spread_w[k] = x

    even = mix[0]
    odd = mix[1]

    def weigh(coef, k, windows):
        pieces = []
        for i, a in enumerate(windows):
            z = coef[32 * i : 32 * i + 32]
            swapped = jnp.concatenate([z[16:], z[:16]], axis=0)
            swapped = jnp.concatenate([swapped[:, 128:], swapped[:, :128]], axis=1)
            w = spread_w[k, a : a + 1, :]
            pieces.append((even * z + odd * swapped) * jnp.concatenate([w, w], axis=1))
        return split(jnp.concatenate(pieces, axis=0))

    def inside_windows(k):
        coef = dot(row_b[...], thrice(first_h[k, 16 : 16 + height], first_l[k, 16 : 16 + height], 0))
        h, l = weigh(coef, k, range(1, win_rows))
        mid_h[k] = h
        mid_l[k] = l

    inner = chunks - 2
    group = 5 if inner % 5 == 0 else 1

    def own_columns(g, carry):
        ks = [1 + g * group + k for k in range(group)]
        columns([(k, 16, 16 + height) for k in ks])
        for k in ks:
            inside_windows(k)
        return carry

    for g in range(inner // group):
        own_columns(g, 0)

    for i in range(8):
        dr, dc = around[i]

        @pl.when(exists(-dr, -dc))
        def _(i=i):
            halo(i).wait_recv()

    rim = [(0, 0, height + 32), (chunks - 1, 0, height + 32)]
    for k in range(1, chunks - 1):
        rim += [(k, 0, 16), (k, 16 + height, 32 + height)]
    columns(rim)
    inside_windows(0)
    inside_windows(chunks - 1)

    def rows_of(k):
        h, l = (jnp.concatenate([x[k, 0:32], x[k, height : height + 32]], axis=0) for x in (first_h, first_l))
        coef = dot(row_rim_b[...], thrice(h, l, 0))
        h, l = weigh(coef, k, (0, win_rows))
        h = jnp.concatenate([h[:32], mid_h[k], h[32:]], axis=0)
        l = jnp.concatenate([l[:32], mid_l[k], l[32:]], axis=0)
        return split(dot(row_back_b[...], thrice(h, l, 0)))

    def chunk_group(ks):
        parts = [rows_of(k) for k in ks]
        h = jnp.concatenate([p[0] for p in parts], axis=0)
        l = jnp.concatenate([p[1] for p in parts], axis=0)
        out = dot(thrice(h, l, 1), col_back3[...])
        for i, k in enumerate(ks):
            start = k * 128 if isinstance(k, int) else pl.multiple_of(k * 128, 128)
            acc[:, pl.ds(start, 256)] += out[i * height : (i + 1) * height]

    def body(g, carry):
        chunk_group([g * group + k for k in range(group)])
        return carry

    for g in range(chunks // group):
        body(g, 0)
    if chunks % group:
        chunk_group(list(range(chunks - chunks % group, chunks)))

    def sums(k, carry):
        lanes = pl.ds(k * 128, 128)
        own = pl.ds(k * 128 + 128, 128)
        d = ext[16 : 16 + height, own]
        e = res[:, lanes]
        q = acc[:, own] + damping * d
        acc[:, own] = q
        terms = (e * e, d * q, e * q, q * q)
        return tuple(t + jnp.sum(v.reshape(-1, 8, 128), axis=0) for t, v in zip(carry, terms))

    zero = jnp.zeros((8, 128), jnp.float32)
    totals = (zero,) * 4
    for k in range(breadth // 128):
        totals = sums(k, totals)
    store = pltpu.make_async_copy(acc.at[:, 128 : 128 + breadth], applied_out, local_sem.at[len(places)])
    store.start()

    tile = jnp.zeros((8, 128), jnp.float32)
    for i, t in enumerate(totals):
        tile = jnp.where(sub == i, jnp.sum(t, axis=0, keepdims=True), tile)

    def exchange(n, me, target, slots, sends, recvs):
        for k in range(1, n):
            to = lax.rem(me + k, n)
            pltpu.make_async_remote_copy(
                src_ref=part,
                dst_ref=slots.at[me],
                send_sem=sends.at[k - 1],
                recv_sem=recvs.at[me],
                device_id=target(to),
                device_id_type=MESH,
            ).start()
        slots[me] = part[...]
        for k in range(1, n):
            source = lax.rem(me + k, n)
            pltpu.make_async_remote_copy(
                src_ref=part,
                dst_ref=slots.at[source],
                send_sem=sends.at[k - 1],
                recv_sem=recvs.at[source],
                device_id=target(source),
                device_id_type=MESH,
            ).wait()
        total = slots[0]
        for k in range(1, n):
            total = total + slots[k]
        return total

    part[...] = tile
    tile = exchange(n_col, c, lambda to: (r, to), red_col, col_send, col_recv)
    part[...] = tile
    tile = exchange(n_row, r, lambda to: (to, c), red_row, row_send, row_recv)

    total = jnp.sum(tile, axis=1, keepdims=True)
    norm_now, curvature, cross, image = (jnp.broadcast_to(total[i : i + 1], (1, 128)) for i in range(4))
    step_length = norm_now / curvature
    norm_next = norm_now - 2.0 * step_length * cross + step_length * step_length * image
    scalars[0:1, :] = step_length
    scalars[1:2, :] = norm_next / norm_now
    scalars[2:8, :] = jnp.zeros((6, 128), jnp.float32)

    for i in range(8):

        @pl.when(exists(*around[i]))
        def _(i=i):
            halo(i).wait_send()

    for i in range(3):

        @pl.when(exists(*forward[i]))
        def _(i=i):
            weights(i).wait_send()

    store.wait()


def update_kernel(
    scalars, iterate, residual, direction, applied, new_iterate, new_residual, new_direction, held, made, sem_in, sem_out
):
    parts = 4
    rows = iterate.shape[0] // parts
    fetches, stores = [], []
    for p in range(parts):
        here = pl.ds(p * rows, rows)
        for i, x in enumerate((direction, iterate, residual, applied)):
            fetches.append(pltpu.make_async_copy(x.at[here], held.at[i, here], sem_in.at[p, i]))
        for i, x in enumerate((new_iterate, new_residual, new_direction)):
            stores.append(pltpu.make_async_copy(made.at[i, here], x.at[here], sem_out.at[p, i]))
    for fetch in fetches:
        fetch.start()
    step_length = scalars[0:1, 0:1]
    ratio = scalars[1:2, 0:1]
    for p in range(parts):
        here = pl.ds(p * rows, rows)
        for fetch in fetches[4 * p : 4 * p + 4]:
            fetch.wait()
        d = held[0, here]
        made[0, here] = held[1, here] + step_length * d
        rest = held[2, here] - step_length * held[3, here]
        made[1, here] = rest
        made[2, here] = rest + ratio * d
        for store in stores[3 * p : 3 * p + 3]:
            store.start()
    for store in stores:
        store.wait()


def per_device(n_row, n_col, iterate, residual, direction, window_weight, freq_weight):
    height, breadth = direction.shape
    win_rows = height // 16
    chunks = breadth // 128 + 1
    operands = (direction, residual, window_weight, freq_weight) + host_tables(win_rows)
    vmem = pl.BlockSpec(memory_space=pltpu.VMEM)
    hbm = pl.BlockSpec(memory_space=pl.ANY)
    dma = pltpu.SemaphoreType.DMA
    f32 = jnp.float32
    applied, scalars = pl.pallas_call(
        functools.partial(kernel, n_row, n_col),
        out_shape=(jax.ShapeDtypeStruct((height, breadth), f32), jax.ShapeDtypeStruct((8, 128), f32)),
        in_specs=[hbm] * len(operands),
        out_specs=(hbm, vmem),
        scratch_shapes=[pltpu.VMEM(x.shape, x.dtype) for x in operands[2:]]
        + [
            pltpu.VMEM((768, 256), jnp.bfloat16),
            pltpu.VMEM((768, 256), jnp.bfloat16),
            pltpu.VMEM((height + 32, breadth + 256), f32),
            pltpu.VMEM((height, breadth), f32),
            pltpu.VMEM((height, breadth + 256), f32),
            pltpu.VMEM((chunks, height + 32, 256), jnp.bfloat16),
            pltpu.VMEM((chunks, height + 32, 256), jnp.bfloat16),
            pltpu.VMEM((chunks, 32 * (win_rows - 1), 256), jnp.bfloat16),
            pltpu.VMEM((chunks, 32 * (win_rows - 1), 256), jnp.bfloat16),
        ]
        + [pltpu.VMEM(x.shape, jnp.bfloat16) for x in operands[6:9]]
        + [
            pltpu.VMEM((8, 128), f32),
            pltpu.VMEM((3, 8, 128), f32),
            pltpu.VMEM((chunks, 8, 128), f32),
            pltpu.VMEM((2, 32, 256), f32),
            pltpu.VMEM((n_col, 8, 128), f32),
            pltpu.VMEM((n_row, 8, 128), f32),
            pltpu.VMEM((8, 128), f32),
            dma((len(operands) + 1,)),
            dma((8,)),
            dma((8,)),
            dma((3,)),
            dma((3,)),
            dma((n_col,)),
            dma((n_col,)),
            dma((n_row,)),
            dma((n_row,)),
        ],
        compiler_params=pltpu.CompilerParams(
            collective_id=0, has_side_effects=True, vmem_limit_bytes=60 * 1024 * 1024
        ),
        cost_estimate=pl.CostEstimate(flops=5_000_000_000, bytes_accessed=2_000_000, transcendentals=0),
    )(*operands)
    return pl.pallas_call(
        update_kernel,
        out_shape=(jax.ShapeDtypeStruct((height, breadth), f32),) * 3,
        in_specs=[vmem] + [hbm] * 4,
        out_specs=(hbm,) * 3,
        scratch_shapes=[
            pltpu.VMEM((4, height, breadth), f32),
            pltpu.VMEM((3, height, breadth), f32),
            dma((4, 4)),
            dma((4, 3)),
        ],
        compiler_params=pltpu.CompilerParams(vmem_limit_bytes=60 * 1024 * 1024),
    )(scalars, iterate, residual, direction, applied)


def solution(mesh):
    return jax.shard_map(
        functools.partial(per_device, mesh.shape["row"], mesh.shape["col"]),
        mesh=mesh,
        in_specs=(P("row", "col"), P("row", "col"), P("row", "col"), P("row", "col"), P()),
        out_specs=(P("row", "col"), P("row", "col"), P("row", "col")),
        check_vma=False,
    )
```

```python
import functools

import jax
import jax.numpy as jnp
import ml_dtypes
import numpy as np
from jax import lax
from jax.experimental import pallas as pl
from jax.experimental.pallas import tpu as pltpu
from jax.sharding import PartitionSpec as P

MESH = pl.DeviceIdType.MESH
damping = 0.5


def split_host(table, axis):
    table = np.asarray(table, np.float32)
    high = table.astype(ml_dtypes.bfloat16)
    low = (table - high.astype(np.float32)).astype(ml_dtypes.bfloat16)
    return jnp.asarray(np.concatenate([high, high, low], axis=axis).astype(np.float32))


def host_tables(win_rows):
    j = np.arange(32)
    window = np.exp(-0.5 * ((j - 15.5) / 8.0) ** 2)
    basis = np.zeros((2, 16, 32))
    for w in range(16):
        phase = 2.0 * np.pi * w * j / 32.0
        basis[0, w] = np.sqrt(2.0) * np.cos(phase) if w else 1.0
        basis[1, w] = np.sqrt(2.0) * np.sin(phase) if w else (-1.0) ** j
    basis = basis * window / np.sqrt(32.0)
    col = np.zeros((256, 2, 16, 8))
    for b in range(8):
        col[112 + 16 * b : 144 + 16 * b, :, :, b] = basis.transpose(2, 0, 1)
    col = col.reshape(256, 256)
    height = 16 * win_rows
    row = np.zeros((32 * (win_rows + 1), height + 32))
    for a in range(win_rows + 1):
        row[32 * a : 32 * a + 32, 16 * a : 16 * a + 32] = basis.reshape(32, 32)
    row_back = row.T[16 : 16 + height]
    even = np.zeros((2, 16, 32))
    odd = np.zeros((2, 16, 32))
    for h in range(2):
        for w in range(16):
            f = 16 if (h == 1 and w == 0) else w
            even[h, w, f] += 0.5
            even[h, w, -f % 32] += 0.5
            sign = 1.0 - 2.0 * h
            odd[h, w, f] += 0.5 * sign
            odd[h, w, -f % 32] -= 0.5 * sign
    even, odd = even.reshape(32, 32), odd.reshape(32, 32)
    left = np.stack([even, -odd]).astype(np.float32)
    right = np.stack([np.repeat(even.T, 8, axis=1), np.repeat(odd.T, 8, axis=1)]).astype(np.float32)
    tables = (jnp.asarray(col, jnp.float32), jnp.asarray(col.T, jnp.float32))
    rim = np.r_[0:32, height : height + 32]
    rim_windows = np.r_[0:32, 32 * win_rows : 32 * win_rows + 32]
    inside = row[32 : 32 * win_rows, 16 : 16 + height]
    tables = tables + (split_host(inside, 1), split_host(row[rim_windows][:, rim], 1), split_host(row_back, 1))
    return tables + (jnp.asarray(left), jnp.asarray(right))


def split(value):
    high = value.astype(jnp.bfloat16)
    low = (value - high.astype(jnp.float32)).astype(jnp.bfloat16)
    return high, low


def thrice(high, low, axis):
    return jnp.concatenate([high, low, high], axis=axis)


def dot(x, y):
    return jnp.dot(x, y, preferred_element_type=jnp.float32)


def kernel(
    n_row,
    n_col,
    direction,
    residual,
    weight_in,
    freq_in,
    col_in,
    col_back_in,
    row_in,
    row_rim_in,
    row_back_in,
    left_in,
    right_in,
    applied_out,
    scalars,
    weight,
    freq,
    col,
    col_back,
    row,
    row_rim,
    row_back,
    left,
    right,
    col3,
    col_back3,
    ext,
    res,
    acc,
    first_h,
    first_l,
    mid_h,
    mid_l,
    row_b,
    row_rim_b,
    row_back_b,
    own_w,
    got_w,
    spread_w,
    mix,
    red_col,
    red_row,
    part,
    local_sem,
    halo_send,
    halo_recv,
    w_send,
    w_recv,
    col_send,
    col_recv,
    row_send,
    row_recv,
):
    r = lax.axis_index("row")
    c = lax.axis_index("col")
    height, breadth = direction.shape
    win_rows = height // 16
    chunks = breadth // 128 + 1

    places = (
        (weight_in, weight),
        (direction, ext.at[16 : 16 + height, 128 : 128 + breadth]),
        (col_in, col),
        (freq_in, freq),
        (left_in, left),
        (right_in, right),
        (row_in, row),
        (row_rim_in, row_rim),
        (residual, res),
        (row_back_in, row_back),
        (col_back_in, col_back),
    )
    fetches = [pltpu.make_async_copy(a, b, local_sem.at[i]) for i, (a, b) in enumerate(places)]

    def exists(dr, dc):
        ok = jnp.bool_(True)
        if dr == 1:
            ok = r < n_row - 1
        if dr == -1:
            ok = r > 0
        if dc == 1:
            ok = jnp.logical_and(ok, c < n_col - 1)
        if dc == -1:
            ok = jnp.logical_and(ok, c > 0)
        return ok

    around = [(dr, dc) for dr in (0, -1, 1) for dc in (0, -1, 1) if (dr, dc) != (0, 0)]

    barrier = pltpu.get_barrier_semaphore()
    for k in range(1, n_col):
        pl.semaphore_signal(barrier, inc=1, device_id=(r, lax.rem(c + k, n_col)), device_id_type=MESH)
    for k in range(1, n_row):
        pl.semaphore_signal(barrier, inc=1, device_id=(lax.rem(r + k, n_row), c), device_id_type=MESH)
    for dr, dc in around:
        if dr != 0 and dc != 0:

            @pl.when(exists(dr, dc))
            def _(dr=dr, dc=dc):
                pl.semaphore_signal(barrier, inc=1, device_id=(r + dr, c + dc), device_id_type=MESH)

    vertical = jnp.where(r > 0, 1, 0) + jnp.where(r < n_row - 1, 1, 0)
    horizontal = jnp.where(c > 0, 1, 0) + jnp.where(c < n_col - 1, 1, 0)

    for fetch in fetches:
        fetch.start()

    own_w[...] = jnp.zeros_like(own_w)
    fetches[0].wait()
    own_w[0:win_rows, :] = weight[...]

    pl.semaphore_wait(barrier, n_col - 1 + n_row - 1 + vertical * horizontal)

    src_rows = {0: slice(0, height), -1: slice(0, 16), 1: slice(height - 16, height)}
    src_cols = {0: slice(0, breadth), -1: slice(0, 128), 1: slice(breadth - 128, breadth)}
    dst_rows = {0: slice(16, 16 + height), -1: slice(16 + height, 32 + height), 1: slice(0, 16)}
    dst_cols = {0: slice(128, 128 + breadth), -1: slice(128 + breadth, 256 + breadth), 1: slice(0, 128)}

    def halo(i):
        dr, dc = around[i]
        return pltpu.make_async_remote_copy(
            src_ref=direction.at[src_rows[dr], src_cols[dc]],
            dst_ref=ext.at[dst_rows[dr], dst_cols[dc]],
            send_sem=halo_send.at[i],
            recv_sem=halo_recv.at[i],
            device_id=(r + dr, c + dc),
            device_id_type=MESH,
        )

    forward = [(0, 1), (1, 0), (1, 1)]

    def weights(i):
        dr, dc = forward[i]
        return pltpu.make_async_remote_copy(
            src_ref=own_w,
            dst_ref=got_w.at[i],
            send_sem=w_send.at[i],
            recv_sem=w_recv.at[i],
            device_id=(r + dr, c + dc),
            device_id_type=MESH,
        )

    for i in range(3):

        @pl.when(exists(*forward[i]))
        def _(i=i):
            weights(i).start()

    order = sorted(range(8), key=lambda i: around[i][1] != 0)
    for i in order:

        @pl.when(exists(*around[i]))
        def _(i=i):
            halo(i).start()

    for i, (dr, dc) in enumerate(around):

        @pl.when(jnp.logical_not(exists(-dr, -dc)))
        def _(dr=dr, dc=dc):
            rows, cols = dst_rows[dr], dst_cols[dc]
            ext[rows, cols] = jnp.zeros((rows.stop - rows.start, cols.stop - cols.start), jnp.float32)

    for i, (dr, dc) in enumerate(forward):

        @pl.when(jnp.logical_not(exists(-dr, -dc)))
        def _(i=i):
            got_w[i] = jnp.zeros_like(own_w)

    acc[...] = jnp.zeros_like(acc)
    def stack_split(table, stack):
        size = table.shape[0]
        h, l = split(table[...])
        stack[0:size, :] = h
        stack[size : 2 * size, :] = h
        stack[2 * size :, :] = l

    fetches[2].wait()
    stack_split(col, col3)
    fetches[1].wait()

    def columns(regions):
        high, low = [], []
        for k, top, end in regions:
            start = k * 128 if isinstance(k, int) else pl.multiple_of(k * 128, 128)
            h, l = split(ext[top:end, pl.ds(start, 256)])
            high.append(h)
            low.append(l)
        high, low = jnp.concatenate(high, axis=0), jnp.concatenate(low, axis=0)
        h, l = split(dot(thrice(high, low, 1), col3[...]))
        at = 0
        for k, top, end in regions:
            first_h[k, top:end, :] = h[at : at + end - top]
            first_l[k, top:end, :] = l[at : at + end - top]
            at += end - top

    inner = chunks - 2
    group = 5 if inner % 5 == 0 else 1
    for g in range(inner // group):
        columns([(1 + g * group + k, 16, 16 + height) for k in range(group)])

    for i in range(3, len(fetches)):
        fetches[i].wait()
    stack_split(col_back, col_back3)
    for table, cast in ((row, row_b), (row_rim, row_rim_b), (row_back, row_back_b)):
        cast[...] = table[...].astype(jnp.bfloat16)
    for m in range(2):
        folded = jnp.dot(left[m], freq[...], precision=lax.Precision.HIGHEST, preferred_element_type=jnp.float32)
        mix[m] = jnp.dot(folded, right[m], precision=lax.Precision.HIGHEST, preferred_element_type=jnp.float32)

    for i in range(3):
        dr, dc = forward[i]

        @pl.when(exists(-dr, -dc))
        def _(i=i):
            weights(i).wait_recv()

    lane = lax.broadcasted_iota(jnp.int32, (8, 128), 1)
    sub = lax.broadcasted_iota(jnp.int32, (8, 128), 0)

    def stacked(above, here):
        return jnp.where(sub == 0, pltpu.roll(above, 8 - (win_rows - 1), 0), pltpu.roll(here, 1, 0))

    main_w = pltpu.roll(stacked(got_w[1], own_w[...]), 1, 1)
    left_w = pltpu.roll(stacked(got_w[2], got_w[0]), 1, 1)
    shifted = jnp.where(lane == 0, left_w, main_w)
    for k in range(chunks):
        if k == chunks - 1:
            x = jnp.where(lane == 0, main_w, 0.0)
        else:
            x = jnp.where(lane < 8, pltpu.roll(shifted, (128 - 8 * k) % 128, 1) if k else shifted, 0.0)
        for step in (8, 16, 32, 64):
            x = x + pltpu.roll(x, step, 1)
        spread_w[k] = x

    even = mix[0]
    odd = mix[1]

    def weigh(coef, k, windows):
        pieces = []
        for i, a in enumerate(windows):
            z = coef[32 * i : 32 * i + 32]
            swapped = jnp.concatenate([z[16:], z[:16]], axis=0)
            swapped = jnp.concatenate([swapped[:, 128:], swapped[:, :128]], axis=1)
            w = spread_w[k, a : a + 1, :]
            pieces.append((even * z + odd * swapped) * jnp.concatenate([w, w], axis=1))
        return split(jnp.concatenate(pieces, axis=0))

    def inside_windows(k):
        coef = dot(row_b[...], thrice(first_h[k, 16 : 16 + height], first_l[k, 16 : 16 + height], 0))
        h, l = weigh(coef, k, range(1, win_rows))
        mid_h[k] = h
        mid_l[k] = l

    def own_windows(g, carry):
        ks = [1 + g * group + k for k in range(group)]
        for k in ks:
            inside_windows(k)
        return carry

    for g in range(inner // group):
        own_windows(g, 0)

    for i in range(8):
        dr, dc = around[i]

        @pl.when(exists(-dr, -dc))
        def _(i=i):
            halo(i).wait_recv()

    rim = [(0, 0, height + 32), (chunks - 1, 0, height + 32)]
    for k in range(1, chunks - 1):
        rim += [(k, 0, 16), (k, 16 + height, 32 + height)]
    columns(rim)
    inside_windows(0)
    inside_windows(chunks - 1)

    def rows_of(k):
        h, l = (jnp.concatenate([x[k, 0:32], x[k, height : height + 32]], axis=0) for x in (first_h, first_l))
        coef = dot(row_rim_b[...], thrice(h, l, 0))
        h, l = weigh(coef, k, (0, win_rows))
        h = jnp.concatenate([h[:32], mid_h[k], h[32:]], axis=0)
        l = jnp.concatenate([l[:32], mid_l[k], l[32:]], axis=0)
        return split(dot(row_back_b[...], thrice(h, l, 0)))

    def chunk_group(ks):
        parts = [rows_of(k) for k in ks]
        h = jnp.concatenate([p[0] for p in parts], axis=0)
        l = jnp.concatenate([p[1] for p in parts], axis=0)
        out = dot(thrice(h, l, 1), col_back3[...])
        for i, k in enumerate(ks):
            start = k * 128 if isinstance(k, int) else pl.multiple_of(k * 128, 128)
            acc[:, pl.ds(start, 256)] += out[i * height : (i + 1) * height]

    def body(g, carry):
        chunk_group([g * group + k for k in range(group)])
        return carry

    for g in range(chunks // group):
        body(g, 0)
    if chunks % group:
        chunk_group(list(range(chunks - chunks % group, chunks)))

    def sums(k, carry):
        lanes = pl.ds(k * 128, 128)
        own = pl.ds(k * 128 + 128, 128)
        d = ext[16 : 16 + height, own]
        e = res[:, lanes]
        q = acc[:, own] + damping * d
        acc[:, own] = q
        terms = (e * e, d * q, e * q, q * q)
        return tuple(t + jnp.sum(v.reshape(-1, 8, 128), axis=0) for t, v in zip(carry, terms))

    zero = jnp.zeros((8, 128), jnp.float32)
    totals = (zero,) * 4
    for k in range(breadth // 128):
        totals = sums(k, totals)
    store = pltpu.make_async_copy(acc.at[:, 128 : 128 + breadth], applied_out, local_sem.at[len(places)])
    store.start()

    tile = jnp.zeros((8, 128), jnp.float32)
    for i, t in enumerate(totals):
        tile = jnp.where(sub == i, jnp.sum(t, axis=0, keepdims=True), tile)

    def exchange(n, me, target, slots, sends, recvs):
        for k in range(1, n):
            to = lax.rem(me + k, n)
            pltpu.make_async_remote_copy(
                src_ref=part,
                dst_ref=slots.at[me],
                send_sem=sends.at[k - 1],
                recv_sem=recvs.at[me],
                device_id=target(to),
                device_id_type=MESH,
            ).start()
        slots[me] = part[...]
        for k in range(1, n):
            source = lax.rem(me + k, n)
            pltpu.make_async_remote_copy(
                src_ref=part,
                dst_ref=slots.at[source],
                send_sem=sends.at[k - 1],
                recv_sem=recvs.at[source],
                device_id=target(source),
                device_id_type=MESH,
            ).wait()
        total = slots[0]
        for k in range(1, n):
            total = total + slots[k]
        return total

    part[...] = tile
    tile = exchange(n_col, c, lambda to: (r, to), red_col, col_send, col_recv)
    part[...] = tile
    tile = exchange(n_row, r, lambda to: (to, c), red_row, row_send, row_recv)

    total = jnp.sum(tile, axis=1, keepdims=True)
    norm_now, curvature, cross, image = (jnp.broadcast_to(total[i : i + 1], (1, 128)) for i in range(4))
    step_length = norm_now / curvature
    norm_next = norm_now - 2.0 * step_length * cross + step_length * step_length * image
    scalars[0:1, :] = step_length
    scalars[1:2, :] = norm_next / norm_now
    scalars[2:8, :] = jnp.zeros((6, 128), jnp.float32)

    for i in range(8):

        @pl.when(exists(*around[i]))
        def _(i=i):
            halo(i).wait_send()

    for i in range(3):

        @pl.when(exists(*forward[i]))
        def _(i=i):
            weights(i).wait_send()

    store.wait()


def update_kernel(
    scalars, iterate, residual, direction, applied, new_iterate, new_residual, new_direction, held, made, sem_in, sem_out
):
    parts = 4
    rows = iterate.shape[0] // parts
    fetches, stores = [], []
    for p in range(parts):
        here = pl.ds(p * rows, rows)
        for i, x in enumerate((direction, iterate, residual, applied)):
            fetches.append(pltpu.make_async_copy(x.at[here], held.at[i, here], sem_in.at[p, i]))
        for i, x in enumerate((new_iterate, new_residual, new_direction)):
            stores.append(pltpu.make_async_copy(made.at[i, here], x.at[here], sem_out.at[p, i]))
    for fetch in fetches:
        fetch.start()
    step_length = scalars[0:1, 0:1]
    ratio = scalars[1:2, 0:1]
    for p in range(parts):
        here = pl.ds(p * rows, rows)
        for fetch in fetches[4 * p : 4 * p + 4]:
            fetch.wait()
        d = held[0, here]
        made[0, here] = held[1, here] + step_length * d
        rest = held[2, here] - step_length * held[3, here]
        made[1, here] = rest
        made[2, here] = rest + ratio * d
        for store in stores[3 * p : 3 * p + 3]:
            store.start()
    for store in stores:
        store.wait()


def per_device(n_row, n_col, iterate, residual, direction, window_weight, freq_weight):
    height, breadth = direction.shape
    win_rows = height // 16
    chunks = breadth // 128 + 1
    operands = (direction, residual, window_weight, freq_weight) + host_tables(win_rows)
    vmem = pl.BlockSpec(memory_space=pltpu.VMEM)
    hbm = pl.BlockSpec(memory_space=pl.ANY)
    dma = pltpu.SemaphoreType.DMA
    f32 = jnp.float32
    applied, scalars = pl.pallas_call(
        functools.partial(kernel, n_row, n_col),
        out_shape=(jax.ShapeDtypeStruct((height, breadth), f32), jax.ShapeDtypeStruct((8, 128), f32)),
        in_specs=[hbm] * len(operands),
        out_specs=(hbm, vmem),
        scratch_shapes=[pltpu.VMEM(x.shape, x.dtype) for x in operands[2:]]
        + [
            pltpu.VMEM((768, 256), jnp.bfloat16),
            pltpu.VMEM((768, 256), jnp.bfloat16),
            pltpu.VMEM((height + 32, breadth + 256), f32),
            pltpu.VMEM((height, breadth), f32),
            pltpu.VMEM((height, breadth + 256), f32),
            pltpu.VMEM((chunks, height + 32, 256), jnp.bfloat16),
            pltpu.VMEM((chunks, height + 32, 256), jnp.bfloat16),
            pltpu.VMEM((chunks, 32 * (win_rows - 1), 256), jnp.bfloat16),
            pltpu.VMEM((chunks, 32 * (win_rows - 1), 256), jnp.bfloat16),
        ]
        + [pltpu.VMEM(x.shape, jnp.bfloat16) for x in operands[6:9]]
        + [
            pltpu.VMEM((8, 128), f32),
            pltpu.VMEM((3, 8, 128), f32),
            pltpu.VMEM((chunks, 8, 128), f32),
            pltpu.VMEM((2, 32, 256), f32),
            pltpu.VMEM((n_col, 8, 128), f32),
            pltpu.VMEM((n_row, 8, 128), f32),
            pltpu.VMEM((8, 128), f32),
            dma((len(operands) + 1,)),
            dma((8,)),
            dma((8,)),
            dma((3,)),
            dma((3,)),
            dma((n_col,)),
            dma((n_col,)),
            dma((n_row,)),
            dma((n_row,)),
        ],
        compiler_params=pltpu.CompilerParams(
            collective_id=0, has_side_effects=True, vmem_limit_bytes=60 * 1024 * 1024
        ),
        cost_estimate=pl.CostEstimate(flops=5_000_000_000, bytes_accessed=2_000_000, transcendentals=0),
    )(*operands)
    return pl.pallas_call(
        update_kernel,
        out_shape=(jax.ShapeDtypeStruct((height, breadth), f32),) * 3,
        in_specs=[vmem] + [hbm] * 4,
        out_specs=(hbm,) * 3,
        scratch_shapes=[
            pltpu.VMEM((4, height, breadth), f32),
            pltpu.VMEM((3, height, breadth), f32),
            dma((4, 4)),
            dma((4, 3)),
        ],
        compiler_params=pltpu.CompilerParams(vmem_limit_bytes=60 * 1024 * 1024),
    )(scalars, iterate, residual, direction, applied)


def solution(mesh):
    return jax.shard_map(
        functools.partial(per_device, mesh.shape["row"], mesh.shape["col"]),
        mesh=mesh,
        in_specs=(P("row", "col"), P("row", "col"), P("row", "col"), P("row", "col"), P()),
        out_specs=(P("row", "col"), P("row", "col"), P("row", "col")),
        check_vma=False,
    )
```
